256 devices in a mesh: member: 4 (over y), slab: 2 (over core), tile: 32 (over x, z).
Axes of the slice: x: 4, y: 4, z: 8, core: 2. Of those that a mesh axis runs over, the one named last changes fastest.
Arguments:
- prior: float32 [128, 262144], P('member', ('slab', 'tile')), may hold values from -6 to 6
- sensitivity: bfloat16 [512, 16, 64, 512], P(('slab', 'tile')), may hold values from -0.0625 to 0.0625
- pattern: int32 [512, 16], P(('slab', 'tile')), may hold values from -1 to 511, as said below
- ownership: int32 [512], replicated, may hold values from 0 to 511, each once
- observed: float32 [32768], P(('slab', 'tile')), may hold values from -8 to 8
- obs_noise: float32 [32768], P(('slab', 'tile')), may hold values from 0.3 to 3
- perturbation: float32 [128, 32768], P('member', ('slab', 'tile')), may hold values from -5 to 5
Outputs:
- increment: float32 [128, 262144], P('member', ('slab', 'tile'))
- weights: float32 [128, 128], replicated
The draws below stay inside these ranges and needn't reach their ends.
Inputs may be any that keep to these rules, and one draw needn't show every extreme that they name: In each row of pattern the first c entries are distinct observation block numbers and the remaining 16 - c entries are -1, with 4 <= c <= 16; some row is full and some row has exactly 4 live entries.
All inputs are finite; a program needn't handle non-finite values.
Results may differ from the reference program's by a relative error of at most 0.0042.
Values may be sent and summed in bfloat16 or wider, within the bound.
A program may use at most 64 MiB of HBM per device.

```python
import math
import jax
import jax.numpy as jnp
from jax import lax

NE = 128
OBS_BLOCK = 64
PB = 512
KB = 16
NPB = 8
OBLK_DEV = 8
NPBT = 512
P_SIZE = 262144
NBLK = 512
M = 32768
N_SLAB = 2
N_TILE = 32


def draw_pattern(key, part):
    row_total = NPB * N_SLAB * N_TILE
    block_total = OBLK_DEV * N_SLAB * N_TILE
    order_key = jax.random.fold_in(key, 11)
    count_key = jax.random.fold_in(key, 12)
    head_key = jax.random.fold_in(key, 13)
    row_keys = jax.random.split(order_key, row_total)
    chosen = jax.vmap(lambda row_key: jax.random.permutation(row_key, block_total)[:KB])(row_keys)
    chosen = chosen.astype(jnp.int32)
    head_row = jnp.concatenate([jnp.full((1,), block_total - 1, jnp.int32), jax.random.permutation(head_key, block_total - 1)[:KB - 1].astype(jnp.int32)])
    chosen = chosen.at[0].set(head_row)
    counts = jax.random.randint(count_key, (row_total,), KB // 4, KB + 1)
    counts = counts.at[0].set(KB).at[row_total - 1].set(KB // 4)
    position = jnp.arange(KB)[None, :]
    return jnp.where(position < counts[:, None], chosen, -1).astype(jnp.int32)


def draw_observed(key, part):
    obs_total = OBLK_DEV * N_SLAB * N_TILE * OBS_BLOCK
    ramp = 0.6 + 1.2 * jnp.arange(obs_total, dtype=jnp.float32) / obs_total
    values = jnp.clip(jax.random.normal(key, (obs_total,), jnp.float32), -4.0, 4.0)
    return (ramp * values).astype(jnp.float32)


def shard_levels(rng, extent, pieces, smallest, largest):
    loudness, own = 1.0, jax.random.fold_in(rng, 6)
    for axis_at, blocks in pieces:
        heights = jnp.exp(jax.random.uniform(jax.random.fold_in(own, axis_at), (blocks,), jnp.float32, smallest / len(pieces), largest / len(pieces)))
        loudness = loudness * jnp.repeat(heights, extent[axis_at] // blocks).reshape([-1 if axis == axis_at else 1 for axis in range(len(extent))])
    return loudness


def scatter_about(stream_key, dims, scale, most, cuts=(), kind=jnp.bfloat16):
    drawn = scale * jax.random.normal(stream_key, dims, jnp.float32)
    if cuts:
        drawn = drawn * shard_levels(stream_key, dims, cuts, -0.22, 0.18)
    return jnp.clip(drawn, -most, most).astype(kind)


def setup_inputs(seed: int = 0) -> dict:
    key_of = jax.random.split(jax.random.key(seed), 8)
    prior = scatter_about(key_of[0], (NE, P_SIZE), 1.0, 6.0, ((0, 4), (1, 64)), jnp.float32)
    sensitivity = scatter_about(key_of[1], (NPBT, KB, OBS_BLOCK, PB), (PB * NPB * KB // OBLK_DEV) ** -0.5, 0.0625, ((0, 64),))
    pattern = draw_pattern(jax.random.fold_in(key_of[7], 71), 0)
    ownership = jax.random.permutation(key_of[3], NBLK).astype(jnp.int32)
    observed = draw_observed(jax.random.fold_in(key_of[7], 71), 0)
    obs_noise = jnp.clip(jnp.exp(math.log(3.0) - 2.3025851 * jax.random.uniform(key_of[5], (M,), jnp.float32) ** shard_levels(key_of[5], (M,), ((0, 64),), -0.2, 0.2)), 0.3, 3.0)
    perturbation = scatter_about(key_of[6], (NE, M), 1.0, 5.0, ((0, 4), (1, 64)), jnp.float32)
    return dict(prior=prior, sensitivity=sensitivity, pattern=pattern, ownership=ownership, observed=observed, obs_noise=obs_noise, perturbation=perturbation)


def reference(prior, sensitivity, pattern, ownership, observed, obs_noise, perturbation):
    group_count = N_SLAB * N_TILE
    prior_bf = prior.astype(jnp.bfloat16)
    shaped = prior_bf.reshape(NE, group_count, NPB, PB).transpose(1, 0, 2, 3)
    sens_groups = sensitivity.reshape(group_count, NPB, KB, OBS_BLOCK, PB)
    pattern_groups = pattern.reshape(group_count, NPB * KB)

    def accumulate_group(carry, item):
        prior_group, sens_group, pattern_group = item
        contrib = jnp.einsum('bkop,mbp->mbko', sens_group.astype(jnp.float32), prior_group.astype(jnp.float32), precision=lax.Precision.HIGHEST)
        contrib = contrib.reshape(NE, NPB * KB, OBS_BLOCK)
        onehot = (pattern_group[:, None] == ownership[None, :]).astype(jnp.float32)
        placed = jnp.einsum('mjo,js->mso', contrib, onehot, precision=lax.Precision.HIGHEST)
        return (carry + placed, None)
    start_value = jnp.zeros((NE, NBLK, OBS_BLOCK), jnp.float32)
    predicted, _ = lax.scan(accumulate_group, start_value, (shaped, sens_groups, pattern_groups))
    predicted = predicted.reshape(NE, M)
    norm_scale = 1.0 / math.sqrt(NE - 1)
    mean_pred = lax.optimization_barrier(jnp.mean(predicted, axis=0))
    spread = (predicted - mean_pred) * norm_scale / obs_noise
    innovation = (observed - predicted) / obs_noise + perturbation
    gram_matrix = jnp.einsum('mo,ko->mk', spread, spread, precision=lax.Precision.HIGHEST)
    cross_term = jnp.einsum('mo,ko->mk', spread, innovation, precision=lax.Precision.HIGHEST)
    misfit = jnp.sum(innovation * innovation)
    damping = misfit / (4.0 * NE * NE)
    system = gram_matrix + damping * jnp.eye(NE, dtype=jnp.float32)
    factor = jnp.linalg.cholesky(system)
    weights = jax.scipy.linalg.cho_solve((factor, True), cross_term)
    centred = ((weights - lax.optimization_barrier(jnp.mean(weights, axis=0, keepdims=True))) * norm_scale).astype(jnp.bfloat16)
    increment = lax.dot_general(centred.astype(jnp.float32), prior_bf.astype(jnp.float32), (((0,), (0,)), ((), ())), preferred_element_type=jnp.float32)
    return (increment, weights)
```

```python
import functools
import math

import jax
import jax.numpy as jnp
from jax import lax
from jax.experimental import pallas as pl
from jax.experimental.pallas import tpu as pltpu
from jax.sharding import PartitionSpec as P

MESH = pl.DeviceIdType.MESH
F32, BF16 = jnp.float32, jnp.bfloat16
HIGHEST = lax.Precision.HIGHEST

NY, NC, NX, NZ = 4, 2, 4, 8
MD = 32
NB, KB, OB, PB = 8, 16, 64, 512
PD = NB * PB
OD = 8 * OB
NE = NY * MD
NT = NX * NZ
NQ = 4
NORM = 1.0 / math.sqrt(NE - 1)


def rows_contract(a, b, precision=None):
    return lax.dot_general(
        a, b, (((1,), (1,)), ((), ())), precision=precision, preferred_element_type=F32
    )


def predict_kernel(
    prior_hbm, sens_hbm, pattern_ref, own_ref, obs_ref, noise_ref, pert_ref,
    sys_ref, prior_all,
    sens_v, prior_v, prior_bf, t_buf, u_buf, pat_buf, onehot, placed, x_in, x_sum, z_in,
    pred, pert_all, s_buf, d_buf, part, ab_in, c_in,
    load_sem, prior_sem, own_sem, g_send, g_recv, u_send, u_recv, x_send, x_recv, z_send, z_recv,
    y_send, y_recv, r_send, r_recv,
):
    y, c, t = lax.axis_index("member"), lax.axis_index("slab"), lax.axis_index("tile")
    x, z = lax.div(t, NZ), lax.rem(t, NZ)

    def wrap(v, n):
        return lax.rem(v, n)

    def device(dy, dc, dx, dz):
        return (wrap(y + dy, NY), wrap(c + dc, NC), wrap(x + dx, NX) * NZ + wrap(z + dz, NZ))

    def send(src, dst, send_sem, recv_sem, to):
        pltpu.make_async_remote_copy(
            src_ref=src, dst_ref=dst, send_sem=send_sem, recv_sem=recv_sem,
            device_id=to, device_id_type=MESH,
        ).start()

    def wait(ref, sem):
        pltpu.make_async_copy(ref, ref, sem).wait()

    load_prior = pltpu.make_async_copy(prior_hbm, prior_v, prior_sem)
    load_prior.start()
    loads = [
        pltpu.make_async_copy(sens_hbm.at[pl.ds(2 * i, 2)], sens_v.at[pl.ds(2 * i, 2)], load_sem.at[i])
        for i in range(NB // 2)
    ]
    for load in loads:
        load.start()

    column = [(dy, dc, dx) for dy in range(NY) for dc in range(NC) for dx in range(NX)][1:]
    barrier = pltpu.get_barrier_semaphore()
    for dy, dc, dx in column:
        pl.semaphore_signal(barrier, inc=1, device_id=device(dy, dc, dx, 0), device_id_type=MESH)
    for dz in range(1, NZ):
        pl.semaphore_signal(barrier, inc=1, device_id=device(0, 0, 0, dz), device_id_type=MESH)

    j = lax.broadcasted_iota(jnp.int32, (KB, 128), 1)
    k = lax.broadcasted_iota(jnp.int32, (KB, 128), 0)
    pick = (k == 2 * (j & 7) + ((j >> 4) & 1)).astype(F32)
    spread_rows = jnp.dot(pattern_ref[...].astype(F32), pick, precision=HIGHEST, preferred_element_type=F32)
    j = lax.broadcasted_iota(jnp.int32, (NB, 128), 1)
    b = lax.broadcasted_iota(jnp.int32, (NB, 128), 0)
    row = jnp.sum(
        jnp.where(b == 2 * (j >> 5) + ((j >> 3) & 1), spread_rows, 0.0), axis=0, keepdims=True
    )
    pat_buf[0] = jnp.broadcast_to(row, (8, 128))

    load_prior.wait()
    prior_bf[...] = prior_v[...].astype(BF16)
    low = lax.broadcasted_iota(jnp.int32, (16, 128), 1) < OB

    for i in range(NB // 2):
        loads[i].wait()
        for b in (2 * i, 2 * i + 1):
            out = rows_contract(
                prior_bf[:, b * PB : (b + 1) * PB], sens_v[b].reshape(KB * OB, PB)
            )
            for kp in range(KB // 2):
                t_buf[pl.ds((b * 8 + kp) * MD, MD), :] = out[:, kp * 128 : (kp + 1) * 128]
        for r in range(MD // 2):
            ta = t_buf[pl.ds(i * 16 * MD + r, 16, stride=MD), :]
            tb = t_buf[pl.ds(i * 16 * MD + r + 16, 16, stride=MD), :]
            lanes = pl.ds((r // 4) * 512 + (r % 2) * 256 + (r // 2 % 2) * 128, 128)
            u_buf[pl.ds(i * 32, 16), lanes] = jnp.where(low, ta, pltpu.roll(tb, OB, 1)).astype(BF16)
            u_buf[pl.ds(i * 32 + 16, 16), lanes] = jnp.where(low, pltpu.roll(ta, OB, 1), tb).astype(BF16)
        if i == 0:
            pl.semaphore_wait(barrier, len(column) + NZ - 1)
            sibling = device(0, 1, 0, 0)
            send(pat_buf.at[0], pat_buf.at[1], u_send.at[4], u_recv.at[4], sibling)
        send(u_buf.at[pl.ds(i * 32, 32)], u_buf.at[pl.ds(128 + i * 32, 32)], u_send.at[i], u_recv.at[i], sibling)
        if i == 0:
            for dy in range(1, NY):
                send(pert_ref, pert_all.at[y], g_send.at[0], g_recv.at[0], device(dy, 0, 0, 0))
            for dy in range(1, NY):
                send(prior_bf, prior_all.at[y], g_send.at[1], g_recv.at[1], device(dy, 0, 0, 0))
            keep_prior = pltpu.make_async_copy(prior_bf, prior_all.at[y], own_sem)
            keep_prior.start()
    pert_all[y] = pert_ref[...]

    wait(pat_buf.at[1], u_recv.at[4])
    for i in range(2):
        owned = own_ref[pl.ds(2 * c + i, 1), :].astype(F32)
        owned = jnp.broadcast_to(owned, (128, 128)).T
        for s in range(2):
            onehot[pl.ds(i * 128, 128), pl.ds(s * 128, 128)] = (
                (owned == pat_buf[s, 0:1, :]).astype(F32).astype(BF16)
            )
    for i in range(NB // 2):
        wait(u_buf.at[pl.ds(128 + i * 32, 32)], u_recv.at[i])

    for q in range(NQ):
        out = jnp.dot(onehot[...], u_buf[:, q * 512 : (q + 1) * 512], preferred_element_type=F32)
        out = jnp.concatenate(
            [out[:, :256].reshape(NT, 8, 256), out[:, 256:].reshape(NT, 8, 256)], axis=1
        )
        placed[q] = out.astype(BF16)
        for dx in range(1, NX):
            send(
                placed.at[q, pl.ds(wrap(x + dx, NX) * NZ, NZ)], x_in.at[q, dx - 1],
                x_send.at[q], x_recv.at[q], device(0, 0, dx, 0),
            )

    def reduce_x(q):
        wait(x_in.at[q], x_recv.at[q])
        total = placed[q, pl.ds(x * NZ, NZ)].astype(F32)
        for d in range(NX - 1):
            total += x_in[q, d].astype(F32)
        x_sum[q] = total.astype(BF16)
        for dz in range(1, NZ):
            send(
                x_sum.at[q, wrap(z + dz, NZ)], z_in.at[q, dz - 1],
                z_send.at[q], z_recv.at[q], device(0, 0, 0, dz),
            )

    def reduce_z(q):
        wait(z_in.at[q], z_recv.at[q])
        total = x_sum[q, z].astype(F32)
        for d in range(NZ - 1):
            total += z_in[q, d].astype(F32)
        first = pl.multiple_of(y * 128 + q * 32, 32)
        for n in range(4):
            h, l = n % 2, n // 2
            pred[pl.ds(first + n * 8, 8), :] = total[h * 8 : (h + 1) * 8, l * 128 : (l + 1) * 128]
        for dy in range(1, NY):
            send(
                pred.at[pl.ds(first, 32)], pred.at[pl.ds(first, 32)],
                y_send.at[q], y_recv.at[q], device(dy, 0, 0, 0),
            )

    for q in range(NQ):
        reduce_x(q)
        if q:
            reduce_z(q - 1)
    reduce_z(NQ - 1)
    wait(pert_all.at[pl.ds(0, NY - 1)], g_recv.at[0])
    for q in range(NQ):
        wait(pred.at[pl.ds(0, 96)], y_recv.at[q])

    low = lax.broadcasted_iota(jnp.int32, (NE // 2, 128), 1) < OB
    misfit = jnp.zeros((1, 1), F32)
    for n in range(OD // 128):
        even = pred[pl.ds(2 * n, NE // 2, stride=8), :]
        odd = pred[pl.ds(2 * n + 1, NE // 2, stride=8), :]
        first = jnp.where(low, even, pltpu.roll(odd, OB, 1))
        second = jnp.where(low, pltpu.roll(even, OB, 1), odd)
        pieces = []
        for w in range(NY):
            pieces += [first[w * 16 : (w + 1) * 16], second[w * 16 : (w + 1) * 16]]
        predicted = jnp.concatenate(pieces, axis=0)
        cols = pl.ds(n * 128, 128)
        noise = noise_ref[:, cols]
        mean = jnp.sum(predicted, axis=0, keepdims=True) / NE
        s_buf[:, cols] = (predicted - mean) * NORM / noise
        innovation = (obs_ref[:, cols] - predicted) / noise + pert_all[:, :, cols].reshape(NE, 128)
        d_buf[:, cols] = innovation
        misfit += jnp.sum(innovation * innovation, axis=(0, 1), keepdims=True)

    half = wrap(y, 2) * 64
    left = s_buf[pl.ds(pl.multiple_of(half, 64), 64), :]
    right = jnp.where(y < 2, s_buf[...], d_buf[...])
    quarter = rows_contract(left, right, HIGHEST)
    r_id = lax.broadcasted_iota(jnp.int32, (64, 128), 0) + half
    c_id = lax.broadcasted_iota(jnp.int32, (64, 128), 1)
    diagonal = jnp.logical_and(r_id == c_id, y < 2)
    quarter = quarter + jnp.where(diagonal, misfit / (4.0 * NE * NE), 0.0)
    part[...] = quarter.reshape(NC * NX, 8, 128)

    me = c * NX + x
    ab_in[me] = part[me]
    for dy, dc, dx in column:
        if dy == 0:
            to = wrap(c + dc, NC) * NX + wrap(x + dx, NX)
            send(part.at[to], ab_in.at[me], r_send.at[0], r_recv.at[0], device(0, dc, dx, 0))
    wait(ab_in.at[pl.ds(0, NC * NX - 1)], r_recv.at[0])
    total = ab_in[0]
    for n in range(1, NC * NX):
        total += ab_in[n]
    c_in[z] = total
    for dz in range(1, NZ):
        send(c_in.at[z], c_in.at[z], r_send.at[1], r_recv.at[1], device(0, 0, 0, dz))
    wait(c_in.at[pl.ds(0, NZ - 1)], r_recv.at[1])
    total = c_in[0]
    for n in range(1, NZ):
        total += c_in[n]
    rows = pl.ds(pl.multiple_of(y * 64 + me * 8, 8), 8)
    sys_ref[rows, :] = total
    for dy, dc, dx in column:
        send(sys_ref.at[rows], sys_ref.at[rows], r_send.at[2], r_recv.at[2], device(dy, dc, dx, 0))
    wait(sys_ref.at[pl.ds(0, 8 * len(column))], r_recv.at[2])

    wait(prior_all.at[pl.ds(0, NY - 1)], g_recv.at[1])
    keep_prior.wait()
    wait(pert_all.at[pl.ds(0, NY - 1)], g_send.at[0])
    wait(prior_all.at[pl.ds(0, NY - 1)], g_send.at[1])
    wait(pat_buf.at[1], u_send.at[4])
    for i in range(NB // 2):
        wait(u_buf.at[pl.ds(128 + i * 32, 32)], u_send.at[i])
    for q in range(NQ):
        wait(x_in.at[q], x_send.at[q])
        wait(z_in.at[q], z_send.at[q])
        wait(pred.at[pl.ds(0, 96)], y_send.at[q])
    wait(ab_in.at[pl.ds(0, NC * NX - 1)], r_send.at[0])
    wait(c_in.at[pl.ds(0, NZ - 1)], r_send.at[1])
    wait(sys_ref.at[pl.ds(0, 8 * len(column))], r_send.at[2])


def solve_kernel(sys_ref, prior_all, inc_ref, weights_ref, prior_v, x_buf, cen_buf, load_sem):
    load = pltpu.make_async_copy(prior_all, prior_v, load_sem)
    load.start()

    def mul(a, b):
        return jnp.dot(a, b, precision=HIGHEST, preferred_element_type=F32)

    system, cross = sys_ref[:NE, :], sys_ref[NE:, :]
    eye = (
        lax.broadcasted_iota(jnp.int32, (NE, NE), 0) == lax.broadcasted_iota(jnp.int32, (NE, NE), 1)
    ).astype(F32)
    bound = jnp.max(jnp.sum(jnp.abs(system), axis=0, keepdims=True), axis=1, keepdims=True)
    x_buf[...] = eye / bound

    def step(carry):
        count, _ = carry
        inverse = x_buf[...]
        residual = eye - mul(sys_ref[:NE, :], inverse)
        x_buf[...] = inverse + mul(inverse, residual)
        return count + 1, jnp.sum(residual * residual)

    lax.while_loop(lambda carry: jnp.logical_and(carry[0] < 48, carry[1] > 1e-7), step, (0, jnp.float32(1.0)))
    inverse = x_buf[...]
    weights = mul(inverse, cross)
    weights = weights + mul(inverse, cross - mul(system, weights))
    weights_ref[...] = weights
    centred = (weights - jnp.sum(weights, axis=0, keepdims=True) / NE) * NORM
    cen_buf[...] = centred.T
    y = lax.axis_index("member")
    own = cen_buf[pl.ds(pl.multiple_of(y * MD, MD), MD), :].astype(BF16)
    load.wait()
    for n in range(8):
        cols = pl.ds(n * 512, 512)
        inc_ref[:, cols] = jnp.dot(own, prior_v[:, :, cols].reshape(NE, 512), preferred_element_type=F32)


def local(prior, sensitivity, pattern, ownership, observed, obs_noise, perturbation):
    vmem, anywhere = pl.BlockSpec(memory_space=pltpu.VMEM), pl.BlockSpec(memory_space=pl.ANY)
    dma = pltpu.SemaphoreType.DMA
    system, prior_all = pl.pallas_call(
        predict_kernel,
        out_shape=(
            jax.ShapeDtypeStruct((2 * NE, NE), F32),
            jax.ShapeDtypeStruct((NY, MD, PD), BF16),
        ),
        in_specs=[anywhere, anywhere] + [vmem] * 5,
        out_specs=(vmem, anywhere),
        scratch_shapes=[
            pltpu.VMEM((NB, KB, OB, PB), BF16),
            pltpu.VMEM((MD, PD), F32),
            pltpu.VMEM((MD, PD), BF16),
            pltpu.VMEM((NB * KB // 2 * MD, 128), F32),
            pltpu.VMEM((256, 2048), BF16),
            pltpu.VMEM((2, 8, 128), F32),
            pltpu.VMEM((256, 256), BF16),
            pltpu.VMEM((NQ, NT, 16, 256), BF16),
            pltpu.VMEM((NQ, NX - 1, NZ, 16, 256), BF16),
            pltpu.VMEM((NQ, NZ, 16, 256), BF16),
            pltpu.VMEM((NQ, NZ - 1, 16, 256), BF16),
            pltpu.VMEM((NY * 128, 128), F32),
            pltpu.VMEM((NY, MD, OD), F32),
            pltpu.VMEM((NE, OD), F32),
            pltpu.VMEM((NE, OD), F32),
            pltpu.VMEM((NC * NX, 8, 128), F32),
            pltpu.VMEM((NC * NX, 8, 128), F32),
            pltpu.VMEM((NZ, 8, 128), F32),
            dma((NB // 2,)), dma, dma,
            dma((2,)), dma((2,)),
            dma((5,)), dma((5,)),
            dma((NQ,)), dma((NQ,)),
            dma((NQ,)), dma((NQ,)),
            dma((NQ,)), dma((NQ,)),
            dma((3,)), dma((3,)),
        ],
        compiler_params=pltpu.CompilerParams(
            collective_id=0, has_side_effects=True, vmem_limit_bytes=40 * 2**20
        ),
        name="predict",
    )(
        prior, sensitivity, pattern, ownership.reshape(4, 128), observed.reshape(1, OD),
        obs_noise.reshape(1, OD), perturbation,
    )
    return pl.pallas_call(
        solve_kernel,
        out_shape=(
            jax.ShapeDtypeStruct((MD, PD), F32),
            jax.ShapeDtypeStruct((NE, NE), F32),
        ),
        in_specs=[vmem, anywhere],
        out_specs=(vmem, vmem),
        scratch_shapes=[
            pltpu.VMEM((NY, MD, PD), BF16),
            pltpu.VMEM((NE, NE), F32),
            pltpu.VMEM((NE, NE), F32),
            dma,
        ],
        compiler_params=pltpu.CompilerParams(vmem_limit_bytes=24 * 2**20),
        name="solve",
    )(system, prior_all)


def solution(mesh):
    return jax.shard_map(
        local,
        mesh=mesh,
        in_specs=(
            P("member", ("slab", "tile")),
            P(("slab", "tile"), None, None, None),
            P(("slab", "tile"), None),
            P(),
            P(("slab", "tile")),
            P(("slab", "tile")),
            P("member", ("slab", "tile")),
        ),
        out_specs=(P("member", ("slab", "tile")), P()),
        check_vma=False,
    )
```

```python
import functools
import math

import jax
import jax.numpy as jnp
from jax import lax
from jax.experimental import pallas as pl
from jax.experimental.pallas import tpu as pltpu
from jax.sharding import PartitionSpec as P

MESH = pl.DeviceIdType.MESH
F32, BF16 = jnp.float32, jnp.bfloat16
HIGHEST = lax.Precision.HIGHEST

NY, NC, NX, NZ = 4, 2, 4, 8
MD = 32
NB, KB, OB, PB = 8, 16, 64, 512
PD = NB * PB
OD = 8 * OB
NE = NY * MD
NT = NX * NZ
NQ = 8
X_FIRST = ((0, 2), (2, 2), (4, 1))
Z_FIRST = ((5, 2), (7, 1))
NORM = 1.0 / math.sqrt(NE - 1)


def rows_contract(a, b, precision=None):
    return lax.dot_general(
        a, b, (((1,), (1,)), ((), ())), precision=precision, preferred_element_type=F32
    )


def predict_kernel(
    prior_hbm, sens_hbm, pattern_hbm, own_hbm, obs_hbm, noise_hbm, pert_hbm,
    sys_ref, prior_all,
    pattern_ref, own_ref, obs_ref, noise_ref, pert_ref,
    sens_v, prior_v, prior_bf, t_buf, u_buf, pat_buf, onehot, placed, x_in, x_own, z_in, z_all, first_sum,
    pred, pert_all, s_buf, d_buf, part, ab_in, c_in,
    load_sem, prior_sem, small_sem, own_sem, g_send, g_recv, u_send, u_recv, x_send, x_recv, z_send, z_recv,
    y_send, y_recv, r_send, r_recv,
):
    y, c, t = lax.axis_index("member"), lax.axis_index("slab"), lax.axis_index("tile")
    x, z = lax.div(t, NZ), lax.rem(t, NZ)

    def wrap(v, n):
        return lax.rem(v, n)

    def device(dy, dc, dx, dz):
        return (wrap(y + dy, NY), wrap(c + dc, NC), wrap(x + dx, NX) * NZ + wrap(z + dz, NZ))

    def send(src, dst, send_sem, recv_sem, to):
        pltpu.make_async_remote_copy(
            src_ref=src, dst_ref=dst, send_sem=send_sem, recv_sem=recv_sem,
            device_id=to, device_id_type=MESH,
        ).start()

    def wait(ref, sem):
        pltpu.make_async_copy(ref, ref, sem).wait()

    arrivals, ends = {}, []

    def expect(name, ref, send_sem, recv_sem):
        arrivals[name] = (ref, recv_sem)
        ends.append((ref, send_sem))

    def arrive(name):
        wait(*arrivals.pop(name))

    def finish():
        for name in list(arrivals):
            arrive(name)
        for pair in ends:
            wait(*pair)
        keep_prior.wait()

    load_prior = pltpu.make_async_copy(prior_hbm, prior_v, prior_sem)
    load_prior.start()
    loads = [
        pltpu.make_async_copy(sens_hbm.at[pl.ds(2 * i, 2)], sens_v.at[pl.ds(2 * i, 2)], load_sem.at[i])
        for i in range(NB // 2)
    ]
    small = [
        pltpu.make_async_copy(src, dst, small_sem.at[i])
        for i, (src, dst) in enumerate((
            (pattern_hbm, pattern_ref), (pert_hbm, pert_ref), (own_hbm, own_ref), (obs_hbm, obs_ref),
            (noise_hbm, noise_ref),
        ))
    ]
    small[0].start()
    for load in loads:
        load.start()
    for load in small[1:]:
        load.start()

    column = [(dy, dc, dx) for dy in range(NY) for dc in range(NC) for dx in range(NX)][1:]
    barrier = pltpu.get_barrier_semaphore()
    for dy, dc, dx in column:
        pl.semaphore_signal(barrier, inc=1, device_id=device(dy, dc, dx, 0), device_id_type=MESH)
    for dz in range(1, NZ):
        pl.semaphore_signal(barrier, inc=1, device_id=device(0, 0, 0, dz), device_id_type=MESH)

    small[0].wait()
    j = lax.broadcasted_iota(jnp.int32, (KB, 128), 1)
    k = lax.broadcasted_iota(jnp.int32, (KB, 128), 0)
    pick = (k == 2 * (j & 7) + ((j >> 4) & 1)).astype(F32)
    spread_rows = jnp.dot(pattern_ref[...].astype(F32), pick, precision=HIGHEST, preferred_element_type=F32)
    j = lax.broadcasted_iota(jnp.int32, (NB, 128), 1)
    b = lax.broadcasted_iota(jnp.int32, (NB, 128), 0)
    row = jnp.sum(
        jnp.where(b == 2 * (j >> 5) + ((j >> 3) & 1), spread_rows, 0.0), axis=0, keepdims=True
    )
    pat_buf[0] = jnp.broadcast_to(row, (8, 128))

    load_prior.wait()
    prior_bf[...] = prior_v[...].astype(BF16)
    low = lax.broadcasted_iota(jnp.int32, (16, 128), 1) < OB

    for i in range(NB // 2):
        loads[i].wait()
        for b in (2 * i, 2 * i + 1):
            out = rows_contract(
                prior_bf[:, b * PB : (b + 1) * PB], sens_v[b].reshape(KB * OB, PB)
            )
            for kp in range(KB // 2):
                t_buf[pl.ds((b * 8 + kp) * MD, MD), :] = out[:, kp * 128 : (kp + 1) * 128]
        for r in range(MD // 2):
            ta = t_buf[pl.ds(i * 16 * MD + r, 16, stride=MD), :]
            tb = t_buf[pl.ds(i * 16 * MD + r + 16, 16, stride=MD), :]
            lanes = pl.ds(r % 2 * 128, 128)
            u_buf[r // 2, pl.ds(i * 32, 16), lanes] = jnp.where(low, ta, pltpu.roll(tb, OB, 1)).astype(BF16)
            u_buf[r // 2, pl.ds(i * 32 + 16, 16), lanes] = jnp.where(low, pltpu.roll(ta, OB, 1), tb).astype(BF16)

    pl.semaphore_wait(barrier, len(column) + NZ - 1)
    sibling = device(0, 1, 0, 0)
    send(pat_buf.at[0], pat_buf.at[1], u_send.at[NQ], u_recv.at[NQ], sibling)
    expect("pattern", pat_buf.at[1], u_send.at[NQ], u_recv.at[NQ])
    for q in range(NQ):
        there = u_buf.at[q, pl.ds(128, 128)]
        send(u_buf.at[q, pl.ds(0, 128)], there, u_send.at[q], u_recv.at[q], sibling)
        expect(("u", q), there, u_send.at[q], u_recv.at[q])
    for load in small[1:]:
        load.wait()
    for dy in range(1, NY):
        send(pert_ref, pert_all.at[y], g_send.at[0], g_recv.at[0], device(dy, 0, 0, 0))
    expect("pert", pert_all.at[pl.ds(0, NY - 1)], g_send.at[0], g_recv.at[0])
    for dy in range(1, NY):
        send(prior_bf, prior_all.at[y], g_send.at[1], g_recv.at[1], device(dy, 0, 0, 0))
    expect("prior", prior_all.at[pl.ds(0, NY - 1)], g_send.at[1], g_recv.at[1])
    keep_prior = pltpu.make_async_copy(prior_bf, prior_all.at[y], own_sem)
    keep_prior.start()
    pert_all[y] = pert_ref[...]

    arrive("pattern")
    for i in range(2):
        owned = own_ref[pl.ds(2 * c + i, 1), :].astype(F32)
        owned = jnp.broadcast_to(owned, (128, 128)).T
        for s in range(2):
            onehot[pl.ds(i * 128, 128), pl.ds(s * 128, 128)] = (
                (owned == pat_buf[s, 0:1, :]).astype(F32).astype(BF16)
            )

    def place(group):
        for q in range(group[0], sum(group)):
            arrive(("u", q))
            out = jnp.dot(onehot[...], u_buf[q], preferred_element_type=F32)
            out = jnp.concatenate(
                [out[:, :128].reshape(NX, NZ, 8, 128), out[:, 128:].reshape(NX, NZ, 8, 128)], axis=2
            )
            placed[q] = out.astype(BF16)

    x_land = {g: (x_in if g in X_FIRST else x_own) for g in X_FIRST + Z_FIRST}
    z_land = {g: (z_all if g in Z_FIRST else z_in) for g in X_FIRST + Z_FIRST}

    def send_x(group):
        qs, land = pl.ds(*group), x_land[group]
        for dx in range(1, NX):
            to = wrap(x + dx, NX)
            src = placed.at[qs, to] if group in X_FIRST else first_sum.at[qs, to]
            send(src, land.at[qs, dx - 1], x_send.at[group[0]], x_recv.at[group[0]], device(0, 0, dx, 0))
        expect(("x", group), land.at[qs], x_send.at[group[0]], x_recv.at[group[0]])

    def send_z(group):
        qs, land = pl.ds(*group), z_land[group]
        for dz in range(1, NZ):
            to = wrap(z + dz, NZ)
            src = placed.at[qs, :, to] if group in Z_FIRST else first_sum.at[qs, to]
            send(src, land.at[qs, dz - 1], z_send.at[group[0]], z_recv.at[group[0]], device(0, 0, 0, dz))
        expect(("z", group), land.at[qs], z_send.at[group[0]], z_recv.at[group[0]])

    def sum_first(group):
        if group in X_FIRST:
            arrive(("x", group))
            for q in range(group[0], sum(group)):
                total = placed[q, x].astype(F32)
                for d in range(NX - 1):
                    total += x_in[q, d].astype(F32)
                first_sum[q] = total.astype(BF16)
            send_z(group)
        else:
            arrive(("z", group))
            for q in range(group[0], sum(group)):
                total = placed[q, :, z].astype(F32)
                for d in range(NZ - 1):
                    total += z_all[q, d].astype(F32)
                first_sum[q, pl.ds(0, NX)] = total.astype(BF16)
            send_x(group)

    def sum_second(group):
        if group in X_FIRST:
            arrive(("z", group))
            parts, own = [z_in.at[:, d] for d in range(NZ - 1)], z
        else:
            arrive(("x", group))
            parts, own = [x_own.at[:, d] for d in range(NX - 1)], x
        for q in range(group[0], sum(group)):
            total = first_sum[q, own].astype(F32)
            for p in parts:
                total += p[q].astype(F32)
            pred[pl.ds(pl.multiple_of(y * 128 + q * 16, 16), 16), :] = total
        rows = pl.ds(pl.multiple_of(y * 128 + group[0] * 16, 16), group[1] * 16)
        for dy in range(1, NY):
            send(pred.at[rows], pred.at[rows], y_send.at[group[0]], y_recv.at[group[0]], device(dy, 0, 0, 0))
        expect(("y", group), pred.at[pl.ds(0, 48 * group[1])], y_send.at[group[0]], y_recv.at[group[0]])

    (xa, xb, xc), (za, zb) = X_FIRST, Z_FIRST
    for group in (xa, za, xb, zb, xc):
        place(group)
        (send_x if group in X_FIRST else send_z)(group)
    sum_first(xa)
    sum_first(xb)
    sum_first(za)
    sum_first(xc)
    sum_second(xa)
    sum_first(zb)
    sum_second(za)
    sum_second(xb)
    sum_second(xc)
    sum_second(zb)
    arrive("pert")
    for group in X_FIRST + Z_FIRST:
        arrive(("y", group))

    low = lax.broadcasted_iota(jnp.int32, (NE // 2, 128), 1) < OB
    misfit = jnp.zeros((1, 1), F32)
    for n in range(OD // 128):
        even = pred[pl.ds(2 * n, NE // 2, stride=8), :]
        odd = pred[pl.ds(2 * n + 1, NE // 2, stride=8), :]
        first = jnp.where(low, even, pltpu.roll(odd, OB, 1))
        second = jnp.where(low, pltpu.roll(even, OB, 1), odd)
        pieces = []
        for w in range(NY):
            pieces += [first[w * 16 : (w + 1) * 16], second[w * 16 : (w + 1) * 16]]
        predicted = jnp.concatenate(pieces, axis=0)
        cols = pl.ds(n * 128, 128)
        noise = noise_ref[:, cols]
        mean = jnp.sum(predicted, axis=0, keepdims=True) / NE
        s_buf[:, cols] = (predicted - mean) * NORM / noise
        innovation = (obs_ref[:, cols] - predicted) / noise + pert_all[:, :, cols].reshape(NE, 128)
        d_buf[:, cols] = innovation
        misfit += jnp.sum(innovation * innovation, axis=(0, 1), keepdims=True)

    half = wrap(y, 2) * 64
    left = s_buf[pl.ds(pl.multiple_of(half, 64), 64), :]
    right = jnp.where(y < 2, s_buf[...], d_buf[...])
    quarter = rows_contract(left, right, HIGHEST)
    r_id = lax.broadcasted_iota(jnp.int32, (64, 128), 0) + half
    c_id = lax.broadcasted_iota(jnp.int32, (64, 128), 1)
    diagonal = jnp.logical_and(r_id == c_id, y < 2)
    quarter = quarter + jnp.where(diagonal, misfit / (4.0 * NE * NE), 0.0)
    part[...] = quarter.reshape(NC * NX, 8, 128)

    me = c * NX + x
    ab_in[me] = part[me]
    for dy, dc, dx in column:
        if dy == 0:
            to = wrap(c + dc, NC) * NX + wrap(x + dx, NX)
            send(part.at[to], ab_in.at[me], r_send.at[0], r_recv.at[0], device(0, dc, dx, 0))
    expect("ab", ab_in.at[pl.ds(0, NC * NX - 1)], r_send.at[0], r_recv.at[0])
    arrive("ab")
    total = ab_in[0]
    for n in range(1, NC * NX):
        total += ab_in[n]
    c_in[z] = total
    for dz in range(1, NZ):
        send(c_in.at[z], c_in.at[z], r_send.at[1], r_recv.at[1], device(0, 0, 0, dz))
    expect("c", c_in.at[pl.ds(0, NZ - 1)], r_send.at[1], r_recv.at[1])
    arrive("c")
    total = c_in[0]
    for n in range(1, NZ):
        total += c_in[n]
    rows = pl.ds(pl.multiple_of(y * 64 + me * 8, 8), 8)
    sys_ref[rows, :] = total
    for dy, dc, dx in column:
        send(sys_ref.at[rows], sys_ref.at[rows], r_send.at[2], r_recv.at[2], device(dy, dc, dx, 0))
    expect("rows", sys_ref.at[pl.ds(0, 8 * len(column))], r_send.at[2], r_recv.at[2])
    arrive("rows")

    finish()


def solve_kernel(sys_ref, prior_all, inc_ref, weights_ref, x_buf, w_buf, cen_buf):
    def mul(a, b):
        return jnp.dot(a, b, precision=HIGHEST, preferred_element_type=F32)

    def rough(a, b):
        return jnp.dot(a.astype(BF16), b.astype(BF16), preferred_element_type=F32)

    system, cross = sys_ref[:NE, :], sys_ref[NE:, :]
    eye = (
        lax.broadcasted_iota(jnp.int32, (NE, NE), 0) == lax.broadcasted_iota(jnp.int32, (NE, NE), 1)
    ).astype(F32)
    bound = jnp.max(jnp.sum(jnp.abs(system), axis=0, keepdims=True), axis=1, keepdims=True)
    start = eye / bound
    inverse = start
    for _ in range(4):
        inverse = inverse + rough(inverse, eye - rough(system, inverse))
    residual = eye - mul(system, inverse)
    x_buf[...] = inverse
    close = jnp.sum(residual * residual)

    @pl.when(jnp.logical_not(close < 0.01))
    def _():
        x_buf[...] = start

        def step(carry):
            count, _ = carry
            inverse = x_buf[...]
            residual = eye - mul(sys_ref[:NE, :], inverse)
            x_buf[...] = inverse + mul(inverse, residual)
            return count + 1, jnp.sum(residual * residual)

        lax.while_loop(
            lambda carry: jnp.logical_and(carry[0] < 64, carry[1] > 1e-7), step, (0, jnp.float32(1.0))
        )

    w_buf[...] = mul(x_buf[...], cross)
    scale = jnp.sum(cross * cross)

    def refine(carry):
        count, _ = carry
        residual = sys_ref[NE:, :] - mul(sys_ref[:NE, :], w_buf[...])
        w_buf[...] += mul(x_buf[...], residual)
        return count + 1, jnp.sum(residual * residual)

    enough = 1e-12 / jnp.minimum(close, 0.01)
    lax.while_loop(
        lambda carry: jnp.logical_and(carry[0] < 12, carry[1] > enough * scale), refine, (0, 2.0 * enough * scale)
    )
    weights = w_buf[...]
    weights_ref[...] = weights
    centred = (weights - jnp.sum(weights, axis=0, keepdims=True) / NE) * NORM
    cen_buf[...] = centred.T
    y = lax.axis_index("member")
    own = cen_buf[pl.ds(pl.multiple_of(y * MD, MD), MD), :].astype(BF16)
    for n in range(8):
        cols = pl.ds(n * 512, 512)
        inc_ref[:, cols] = jnp.dot(own, prior_all[:, :, cols].reshape(NE, 512), preferred_element_type=F32)


def local(prior, sensitivity, pattern, ownership, observed, obs_noise, perturbation):
    vmem, anywhere = pl.BlockSpec(memory_space=pltpu.VMEM), pl.BlockSpec(memory_space=pl.ANY)
    hbm = pl.BlockSpec(memory_space=pltpu.HBM)
    dma = pltpu.SemaphoreType.DMA
    operands = [
        pltpu.with_memory_space_constraint(a, pltpu.HBM)
        for a in (
            prior, sensitivity, pattern, ownership.reshape(4, 128), observed.reshape(1, OD),
            obs_noise.reshape(1, OD), perturbation,
        )
    ]
    system, prior_all = pl.pallas_call(
        predict_kernel,
        out_shape=(
            jax.ShapeDtypeStruct((2 * NE, NE), F32),
            jax.ShapeDtypeStruct((NY, MD, PD), BF16),
        ),
        in_specs=[hbm] * 7,
        out_specs=(vmem, anywhere),
        scratch_shapes=[
            pltpu.VMEM((NB, KB), jnp.int32),
            pltpu.VMEM((4, 128), jnp.int32),
            pltpu.VMEM((1, OD), F32),
            pltpu.VMEM((1, OD), F32),
            pltpu.VMEM((MD, OD), F32),
            pltpu.VMEM((NB, KB, OB, PB), BF16),
            pltpu.VMEM((MD, PD), F32),
            pltpu.VMEM((MD, PD), BF16),
            pltpu.VMEM((NB * KB // 2 * MD, 128), F32),
            pltpu.VMEM((NQ, 256, 256), BF16),
            pltpu.VMEM((2, 8, 128), F32),
            pltpu.VMEM((256, 256), BF16),
            pltpu.VMEM((NQ, NX, NZ, 16, 128), BF16),
            pltpu.VMEM((NQ, NX - 1, NZ, 16, 128), BF16),
            pltpu.VMEM((NQ, NX - 1, 16, 128), BF16),
            pltpu.VMEM((NQ, NZ - 1, 16, 128), BF16),
            pltpu.VMEM((NQ, NZ - 1, NX, 16, 128), BF16),
            pltpu.VMEM((NQ, NZ, 16, 128), BF16),
            pltpu.VMEM((NY * 128, 128), F32),
            pltpu.VMEM((NY, MD, OD), F32),
            pltpu.VMEM((NE, OD), F32),
            pltpu.VMEM((NE, OD), F32),
            pltpu.VMEM((NC * NX, 8, 128), F32),
            pltpu.VMEM((NC * NX, 8, 128), F32),
            pltpu.VMEM((NZ, 8, 128), F32),
            dma((NB // 2,)), dma, dma((5,)), dma,
            dma((2,)), dma((2,)),
            dma((NQ + 1,)), dma((NQ + 1,)),
            dma((NQ,)), dma((NQ,)),
            dma((NQ,)), dma((NQ,)),
            dma((NQ,)), dma((NQ,)),
            dma((3,)), dma((3,)),
        ],
        compiler_params=pltpu.CompilerParams(
            collective_id=0, has_side_effects=True, vmem_limit_bytes=40 * 2**20
        ),
        name="predict",
    )(*operands)
    return pl.pallas_call(
        solve_kernel,
        out_shape=(
            jax.ShapeDtypeStruct((MD, PD), F32),
            jax.ShapeDtypeStruct((NE, NE), F32),
        ),
        in_specs=[vmem, vmem],
        out_specs=(vmem, vmem),
        scratch_shapes=[
            pltpu.VMEM((NE, NE), F32),
            pltpu.VMEM((NE, NE), F32),
            pltpu.VMEM((NE, NE), F32),
        ],
        compiler_params=pltpu.CompilerParams(vmem_limit_bytes=24 * 2**20),
        name="solve",
    )(system, prior_all)


def solution(mesh):
    return jax.shard_map(
        local,
        mesh=mesh,
        in_specs=(
            P("member", ("slab", "tile")),
            P(("slab", "tile"), None, None, None),
            P(("slab", "tile"), None),
            P(),
            P(("slab", "tile")),
            P(("slab", "tile")),
            P("member", ("slab", "tile")),
        ),
        out_specs=(P("member", ("slab", "tile")), P()),
        check_vma=False,
    )
```

```python
import functools
import math

import jax
import jax.numpy as jnp
from jax import lax
from jax.experimental import pallas as pl
from jax.experimental.pallas import tpu as pltpu
from jax.sharding import PartitionSpec as P

MESH = pl.DeviceIdType.MESH
F32, BF16 = jnp.float32, jnp.bfloat16
HIGHEST = lax.Precision.HIGHEST

NY, NC, NX, NZ = 4, 2, 4, 8
MD = 32
NB, KB, OB, PB = 8, 16, 64, 512
PD = NB * PB
OD = 8 * OB
NE = NY * MD
NT = NX * NZ
NQ = 8
X_FIRST, Z_FIRST = ((0, 1), (1, 2), (3, 2), (5, 1)), ((6, 1), (7, 1))
PLACE = ((6, 1), (0, 1), (7, 1), (1, 2), (3, 2), (5, 1))
SUMS = (
    (0, (0, 1)), (0, (6, 1)), (0, (1, 2)), (0, (7, 1)), (0, (3, 2)), (0, (5, 1)),
    (1, (0, 1)), (1, (6, 1)), (1, (1, 2)), (1, (7, 1)), (1, (3, 2)), (1, (5, 1)),
)
NORM = 1.0 / math.sqrt(NE - 1)


def rows_contract(a, b, precision=None):
    return lax.dot_general(
        a, b, (((1,), (1,)), ((), ())), precision=precision, preferred_element_type=F32
    )


def predict_kernel(
    prior_hbm, sens_hbm, pattern_hbm, own_hbm, obs_hbm, noise_hbm, pert_hbm,
    sys_ref, prior_all,
    pattern_ref, own_ref, obs_ref, noise_ref, pert_ref,
    sens_v, prior_v, prior_bf, t_buf, u_buf, pat_buf, owner, onehot, placed, x_in, x_own, z_in, z_all, first_sum,
    pred, pert_all, s_buf, d_buf, part, ab_in, c_in,
    load_sem, prior_sem, small_sem, own_sem, g_send, g_recv, u_send, u_recv, x_send, x_recv, z_send, z_recv,
    y_send, y_recv, r_send, r_recv,
):
    y, c, t = lax.axis_index("member"), lax.axis_index("slab"), lax.axis_index("tile")
    x, z = lax.div(t, NZ), lax.rem(t, NZ)

    def wrap(v, n):
        return lax.rem(v, n)

    def device(dy, dc, dx, dz):
        return (wrap(y + dy, NY), wrap(c + dc, NC), wrap(x + dx, NX) * NZ + wrap(z + dz, NZ))

    def send(src, dst, send_sem, recv_sem, to):
        pltpu.make_async_remote_copy(
            src_ref=src, dst_ref=dst, send_sem=send_sem, recv_sem=recv_sem,
            device_id=to, device_id_type=MESH,
        ).start()

    def wait(ref, sem):
        pltpu.make_async_copy(ref, ref, sem).wait()

    started = set()
    arrivals, ends = {}, []

    def expect(name, ref, send_sem, recv_sem):
        arrivals[name] = (ref, recv_sem)
        started.add(name)
        ends.append((ref, send_sem))

    def arrive(name):
        wait(*arrivals.pop(name))

    def finish():
        for name in list(arrivals):
            arrive(name)
        for pair in ends:
            wait(*pair)
        if "prior" in started:
            keep_prior.wait()

    load_prior = pltpu.make_async_copy(prior_hbm, prior_v, prior_sem)
    load_prior.start()
    loads = [
        pltpu.make_async_copy(sens_hbm.at[pl.ds(2 * i, 2)], sens_v.at[pl.ds(2 * i, 2)], load_sem.at[i])
        for i in range(NB // 2)
    ]
    small = [
        pltpu.make_async_copy(src, dst, small_sem.at[i])
        for i, (src, dst) in enumerate((
            (pattern_hbm, pattern_ref), (pert_hbm, pert_ref), (own_hbm, own_ref), (obs_hbm, obs_ref),
            (noise_hbm, noise_ref),
        ))
    ]
    small[0].start()
    for load in loads:
        load.start()
    for load in small[1:]:
        load.start()

    column = [(dy, dc, dx) for dy in range(NY) for dc in range(NC) for dx in range(NX)][1:]
    barrier = pltpu.get_barrier_semaphore()
    for dy, dc, dx in column:
        pl.semaphore_signal(barrier, inc=1, device_id=device(dy, dc, dx, 0), device_id_type=MESH)
    for dz in range(1, NZ):
        pl.semaphore_signal(barrier, inc=1, device_id=device(0, 0, 0, dz), device_id_type=MESH)

    small[0].wait()
    j = lax.broadcasted_iota(jnp.int32, (KB, 128), 1)
    k = lax.broadcasted_iota(jnp.int32, (KB, 128), 0)
    pick = (k == 2 * (j & 7) + ((j >> 4) & 1)).astype(F32)
    spread_rows = jnp.dot(pattern_ref[...].astype(F32), pick, precision=HIGHEST, preferred_element_type=F32)
    j = lax.broadcasted_iota(jnp.int32, (NB, 128), 1)
    b = lax.broadcasted_iota(jnp.int32, (NB, 128), 0)
    row = jnp.sum(
        jnp.where(b == 2 * (j >> 5) + ((j >> 3) & 1), spread_rows, 0.0), axis=0, keepdims=True
    )
    pat_buf[0] = jnp.broadcast_to(row, (8, 128))

    load_prior.wait()
    prior_bf[...] = prior_v[...].astype(BF16)
    low = lax.broadcasted_iota(jnp.int32, (16, 128), 1) < OB

    for i in range(NB // 2):
        loads[i].wait()
        for b in (2 * i, 2 * i + 1):
            out = rows_contract(
                prior_bf[:, b * PB : (b + 1) * PB], sens_v[b].reshape(KB * OB, PB)
            )
            for kp in range(KB // 2):
                t_buf[pl.ds((b * 8 + kp) * MD, MD), :] = out[:, kp * 128 : (kp + 1) * 128]
        for r in range(MD // 2):
            ta = t_buf[pl.ds(i * 16 * MD + r, 16, stride=MD), :]
            tb = t_buf[pl.ds(i * 16 * MD + r + 16, 16, stride=MD), :]
            lanes = pl.ds(r % 2 * 128, 128)
            u_buf[r // 2, pl.ds(i * 32, 16), lanes] = jnp.where(low, ta, pltpu.roll(tb, OB, 1)).astype(BF16)
            u_buf[r // 2, pl.ds(i * 32 + 16, 16), lanes] = jnp.where(low, pltpu.roll(ta, OB, 1), tb).astype(BF16)

    for load in small[1:]:
        load.wait()
    for i in range(2):
        owned = own_ref[pl.ds(2 * c + i, 1), :].astype(F32)
        owned = jnp.broadcast_to(owned, (128, 128)).T
        owner[pl.ds(i * 128, 128), :] = owned
        onehot[pl.ds(i * 128, 128), pl.ds(0, 128)] = (owned == row).astype(F32).astype(BF16)
    pert_all[y] = pert_ref[...]

    pl.semaphore_wait(barrier, len(column) + NZ - 1)
    sibling = device(0, 1, 0, 0)
    send(pat_buf.at[0], pat_buf.at[1], u_send.at[NQ], u_recv.at[NQ], sibling)
    expect("pattern", pat_buf.at[1], u_send.at[NQ], u_recv.at[NQ])
    for group in PLACE:
        qs, at = pl.ds(*group), group[0]
        there = u_buf.at[qs, pl.ds(128, 128)]
        send(u_buf.at[qs, pl.ds(0, 128)], there, u_send.at[at], u_recv.at[at], sibling)
        expect(("u", group), there, u_send.at[at], u_recv.at[at])
    for dy in range(1, NY):
        send(pert_ref, pert_all.at[y], g_send.at[0], g_recv.at[0], device(dy, 0, 0, 0))
    expect("pert", pert_all.at[pl.ds(0, NY - 1)], g_send.at[0], g_recv.at[0])
    for dy in range(1, NY):
        send(prior_bf, prior_all.at[y], g_send.at[1], g_recv.at[1], device(dy, 0, 0, 0))
    expect("prior", prior_all.at[pl.ds(0, NY - 1)], g_send.at[1], g_recv.at[1])
    keep_prior = pltpu.make_async_copy(prior_bf, prior_all.at[y], own_sem)
    keep_prior.start()
    arrive("pattern")
    onehot[:, pl.ds(128, 128)] = (owner[...] == pat_buf[1, 0:1, :]).astype(F32).astype(BF16)

    def place(group):
        arrive(("u", group))
        for q in range(group[0], sum(group)):
            out = jnp.dot(onehot[...], u_buf[q], preferred_element_type=F32)
            out = jnp.concatenate(
                [out[:, :128].reshape(NX, NZ, 8, 128), out[:, 128:].reshape(NX, NZ, 8, 128)], axis=2
            )
            placed[q] = out.astype(BF16)

    x_land = {g: (x_in if g in X_FIRST else x_own) for g in X_FIRST + Z_FIRST}
    z_land = {g: (z_all if g in Z_FIRST else z_in) for g in X_FIRST + Z_FIRST}

    def send_x(group):
        qs, land = pl.ds(*group), x_land[group]
        for dx in range(1, NX):
            to = wrap(x + dx, NX)
            src = placed.at[qs, to] if group in X_FIRST else first_sum.at[qs, to]
            send(src, land.at[qs, dx - 1], x_send.at[group[0]], x_recv.at[group[0]], device(0, 0, dx, 0))
        expect(("x", group), land.at[qs], x_send.at[group[0]], x_recv.at[group[0]])

    def send_z(group):
        qs, land = pl.ds(*group), z_land[group]
        for dz in range(1, NZ):
            to = wrap(z + dz, NZ)
            src = placed.at[qs, :, to] if group in Z_FIRST else first_sum.at[qs, to]
            send(src, land.at[qs, dz - 1], z_send.at[group[0]], z_recv.at[group[0]], device(0, 0, 0, dz))
        expect(("z", group), land.at[qs], z_send.at[group[0]], z_recv.at[group[0]])

    def sum_first(group):
        if group in X_FIRST:
            arrive(("x", group))
            for q in range(group[0], sum(group)):
                total = placed[q, x].astype(F32)
                for d in range(NX - 1):
                    total += x_in[q, d].astype(F32)
                first_sum[q] = total.astype(BF16)
            send_z(group)
        else:
            arrive(("z", group))
            for q in range(group[0], sum(group)):
                total = placed[q, :, z].astype(F32)
                for d in range(NZ - 1):
                    total += z_all[q, d].astype(F32)
                first_sum[q, pl.ds(0, NX)] = total.astype(BF16)
            send_x(group)

    def sum_second(group):
        if group in X_FIRST:
            arrive(("z", group))
            parts, own = [z_in.at[:, d] for d in range(NZ - 1)], z
        else:
            arrive(("x", group))
            parts, own = [x_own.at[:, d] for d in range(NX - 1)], x
        for q in range(group[0], sum(group)):
            total = first_sum[q, own].astype(F32)
            for p in parts:
                total += p[q].astype(F32)
            pred[pl.ds(pl.multiple_of(y * 128 + q * 16, 16), 16), :] = total
        rows = pl.ds(pl.multiple_of(y * 128 + group[0] * 16, 16), group[1] * 16)
        for dy in range(1, NY):
            send(pred.at[rows], pred.at[rows], y_send.at[group[0]], y_recv.at[group[0]], device(dy, 0, 0, 0))
        expect(("y", group), pred.at[pl.ds(0, 48 * group[1])], y_send.at[group[0]], y_recv.at[group[0]])

    for group in PLACE:
        place(group)
        (send_x if group in X_FIRST else send_z)(group)

    for stage, group in SUMS:
        (sum_second if stage else sum_first)(group)
    arrive("pert")
    for group in X_FIRST + Z_FIRST:
        arrive(("y", group))

    low = lax.broadcasted_iota(jnp.int32, (NE // 2, 128), 1) < OB
    misfit = jnp.zeros((1, 1), F32)
    for n in range(OD // 128):
        even = pred[pl.ds(2 * n, NE // 2, stride=8), :]
        odd = pred[pl.ds(2 * n + 1, NE // 2, stride=8), :]
        first = jnp.where(low, even, pltpu.roll(odd, OB, 1))
        second = jnp.where(low, pltpu.roll(even, OB, 1), odd)
        pieces = []
        for w in range(NY):
            pieces += [first[w * 16 : (w + 1) * 16], second[w * 16 : (w + 1) * 16]]
        predicted = jnp.concatenate(pieces, axis=0)
        cols = pl.ds(n * 128, 128)
        noise = noise_ref[:, cols]
        mean = jnp.sum(predicted, axis=0, keepdims=True) / NE
        s_buf[:, cols] = (predicted - mean) * NORM / noise
        innovation = (obs_ref[:, cols] - predicted) / noise + pert_all[:, :, cols].reshape(NE, 128)
        d_buf[:, cols] = innovation
        misfit += jnp.sum(innovation * innovation, axis=(0, 1), keepdims=True)

    half = wrap(y, 2) * 64
    left = s_buf[pl.ds(pl.multiple_of(half, 64), 64), :]
    right = jnp.where(y < 2, s_buf[...], d_buf[...])
    quarter = rows_contract(left, right, HIGHEST)
    r_id = lax.broadcasted_iota(jnp.int32, (64, 128), 0) + half
    c_id = lax.broadcasted_iota(jnp.int32, (64, 128), 1)
    diagonal = jnp.logical_and(r_id == c_id, y < 2)
    quarter = quarter + jnp.where(diagonal, misfit / (4.0 * NE * NE), 0.0)
    part[...] = quarter.reshape(NC * NX, 8, 128)

    me = c * NX + x
    ab_in[me] = part[me]
    for dy, dc, dx in column:
        if dy == 0:
            to = wrap(c + dc, NC) * NX + wrap(x + dx, NX)
            send(part.at[to], ab_in.at[me], r_send.at[0], r_recv.at[0], device(0, dc, dx, 0))
    expect("ab", ab_in.at[pl.ds(0, NC * NX - 1)], r_send.at[0], r_recv.at[0])
    arrive("ab")
    total = ab_in[0]
    for n in range(1, NC * NX):
        total += ab_in[n]
    c_in[z] = total
    for dz in range(1, NZ):
        send(c_in.at[z], c_in.at[z], r_send.at[1], r_recv.at[1], device(0, 0, 0, dz))
    expect("c", c_in.at[pl.ds(0, NZ - 1)], r_send.at[1], r_recv.at[1])
    arrive("c")
    total = c_in[0]
    for n in range(1, NZ):
        total += c_in[n]
    rows = pl.ds(pl.multiple_of(y * 64 + me * 8, 8), 8)
    sys_ref[rows, :] = total
    for dy, dc, dx in column:
        send(sys_ref.at[rows], sys_ref.at[rows], r_send.at[2], r_recv.at[2], device(dy, dc, dx, 0))
    expect("rows", sys_ref.at[pl.ds(0, 8 * len(column))], r_send.at[2], r_recv.at[2])
    arrive("rows")

    finish()


def solve_kernel(
    sys_ref, prior_all, inc_hbm, weights_hbm, x_buf, w_buf, cen_buf, inc_buf, out_sem
):
    def mul(a, b):
        return jnp.dot(a, b, precision=HIGHEST, preferred_element_type=F32)

    def rough(a, b):
        return jnp.dot(a.astype(BF16), b.astype(BF16), preferred_element_type=F32)

    system, cross = sys_ref[:NE, :], sys_ref[NE:, :]
    eye = (
        lax.broadcasted_iota(jnp.int32, (NE, NE), 0) == lax.broadcasted_iota(jnp.int32, (NE, NE), 1)
    ).astype(F32)
    bound = jnp.max(jnp.sum(jnp.abs(system), axis=0, keepdims=True), axis=1, keepdims=True)
    start = eye / bound
    least = jnp.sum(jnp.sum(system, axis=0, keepdims=True), axis=1, keepdims=True) / NE
    inverse = eye * (2.0 / (bound + jnp.maximum(least, 0.0)))
    for _ in range(3):
        inverse = inverse + rough(inverse, eye - rough(system, inverse))
    residual = eye - mul(system, inverse)
    x_buf[...] = inverse
    close = jnp.sum(residual * residual)

    @pl.when(jnp.logical_not(close < 0.01))
    def _():
        x_buf[...] = start

        def step(carry):
            count, _ = carry
            inverse = x_buf[...]
            residual = eye - mul(sys_ref[:NE, :], inverse)
            x_buf[...] = inverse + mul(inverse, residual)
            return count + 1, jnp.sum(residual * residual)

        lax.while_loop(
            lambda carry: jnp.logical_and(carry[0] < 64, carry[1] > 1e-7), step, (0, jnp.float32(1.0))
        )

    w_buf[...] = mul(x_buf[...], cross)
    scale = jnp.sum(cross * cross)

    def refine(carry):
        count, _ = carry
        residual = sys_ref[NE:, :] - mul(sys_ref[:NE, :], w_buf[...])
        w_buf[...] += mul(x_buf[...], residual)
        return count + 1, jnp.sum(residual * residual)

    enough = 1e-12 / jnp.minimum(close, 0.01)
    lax.while_loop(
        lambda carry: jnp.logical_and(carry[0] < 12, carry[1] > enough * scale), refine, (0, 2.0 * enough * scale)
    )
    weights = w_buf[...]
    stores = [pltpu.make_async_copy(w_buf, weights_hbm, out_sem.at[4])]
    stores[0].start()
    centred = (weights - jnp.sum(weights, axis=0, keepdims=True) / NE) * NORM
    cen_buf[...] = centred.T
    y = lax.axis_index("member")
    own = cen_buf[pl.ds(pl.multiple_of(y * MD, MD), MD), :].astype(BF16)
    for n in range(4):
        cols = pl.ds(n * 1024, 1024)
        inc_buf[n] = jnp.dot(own, prior_all[:, :, cols].reshape(NE, 1024), preferred_element_type=F32)
        stores.append(pltpu.make_async_copy(inc_buf.at[n], inc_hbm.at[:, cols], out_sem.at[n]))
        stores[-1].start()
    for store in stores:
        store.wait()


def local(prior, sensitivity, pattern, ownership, observed, obs_noise, perturbation):
    vmem, anywhere = pl.BlockSpec(memory_space=pltpu.VMEM), pl.BlockSpec(memory_space=pl.ANY)
    hbm = pl.BlockSpec(memory_space=pltpu.HBM)
    dma = pltpu.SemaphoreType.DMA
    operands = [
        pltpu.with_memory_space_constraint(a, pltpu.HBM)
        for a in (
            prior, sensitivity, pattern, ownership.reshape(4, 128), observed.reshape(1, OD),
            obs_noise.reshape(1, OD), perturbation,
        )
    ]
    system, prior_all = pl.pallas_call(
        predict_kernel,
        out_shape=(
            jax.ShapeDtypeStruct((2 * NE, NE), F32),
            jax.ShapeDtypeStruct((NY, MD, PD), BF16),
        ),
        in_specs=[hbm] * 7,
        out_specs=(vmem, anywhere),
        scratch_shapes=[
            pltpu.VMEM((NB, KB), jnp.int32),
            pltpu.VMEM((4, 128), jnp.int32),
            pltpu.VMEM((1, OD), F32),
            pltpu.VMEM((1, OD), F32),
            pltpu.VMEM((MD, OD), F32),
            pltpu.VMEM((NB, KB, OB, PB), BF16),
            pltpu.VMEM((MD, PD), F32),
            pltpu.VMEM((MD, PD), BF16),
            pltpu.VMEM((NB * KB // 2 * MD, 128), F32),
            pltpu.VMEM((NQ, 256, 256), BF16),
            pltpu.VMEM((2, 8, 128), F32),
            pltpu.VMEM((256, 128), F32),
            pltpu.VMEM((256, 256), BF16),
            pltpu.VMEM((NQ, NX, NZ, 16, 128), BF16),
            pltpu.VMEM((NQ, NX - 1, NZ, 16, 128), BF16),
            pltpu.VMEM((NQ, NX - 1, 16, 128), BF16),
            pltpu.VMEM((NQ, NZ - 1, 16, 128), BF16),
            pltpu.VMEM((NQ, NZ - 1, NX, 16, 128), BF16),
            pltpu.VMEM((NQ, NZ, 16, 128), BF16),
            pltpu.VMEM((NY * 128, 128), F32),
            pltpu.VMEM((NY, MD, OD), F32),
            pltpu.VMEM((NE, OD), F32),
            pltpu.VMEM((NE, OD), F32),
            pltpu.VMEM((NC * NX, 8, 128), F32),
            pltpu.VMEM((NC * NX, 8, 128), F32),
            pltpu.VMEM((NZ, 8, 128), F32),
            dma((NB // 2,)), dma, dma((5,)), dma,
            dma((2,)), dma((2,)),
            dma((NQ + 1,)), dma((NQ + 1,)),
            dma((NQ,)), dma((NQ,)),
            dma((NQ,)), dma((NQ,)),
            dma((NQ,)), dma((NQ,)),
            dma((3,)), dma((3,)),
        ],
        compiler_params=pltpu.CompilerParams(
            collective_id=0, has_side_effects=True, vmem_limit_bytes=40 * 2**20
        ),
        name="predict",
    )(*operands)
    return pl.pallas_call(
        solve_kernel,
        out_shape=(
            jax.ShapeDtypeStruct((MD, PD), F32),
            jax.ShapeDtypeStruct((NE, NE), F32),
        ),
        in_specs=[vmem, vmem],
        out_specs=(anywhere, anywhere),
        scratch_shapes=[
            pltpu.VMEM((NE, NE), F32),
            pltpu.VMEM((NE, NE), F32),
            pltpu.VMEM((NE, NE), F32),
            pltpu.VMEM((4, MD, 1024), F32),
            dma((5,)),
        ],
        compiler_params=pltpu.CompilerParams(vmem_limit_bytes=24 * 2**20),
        name="solve",
    )(system, prior_all)


def solution(mesh):
    return jax.shard_map(
        local,
        mesh=mesh,
        in_specs=(
            P("member", ("slab", "tile")),
            P(("slab", "tile"), None, None, None),
            P(("slab", "tile"), None),
            P(),
            P(("slab", "tile")),
            P(("slab", "tile")),
            P("member", ("slab", "tile")),
        ),
        out_specs=(P("member", ("slab", "tile")), P()),
        check_vma=False,
    )
```

```python
import functools
import math

import jax
import jax.numpy as jnp
from jax import lax
from jax.experimental import pallas as pl
from jax.experimental.pallas import tpu as pltpu
from jax.sharding import PartitionSpec as P

MESH = pl.DeviceIdType.MESH
F32, BF16 = jnp.float32, jnp.bfloat16
HIGHEST = lax.Precision.HIGHEST

NY, NC, NX, NZ = 4, 2, 4, 8
MD = 32
NB, KB, OB, PB = 8, 16, 64, 512
PD = NB * PB
OD = 8 * OB
NE = NY * MD
NT = NX * NZ
NQ = 8
X_FIRST, Z_FIRST = ((0, 1), (1, 2), (3, 2), (5, 1)), ((6, 1), (7, 1))
PLACE = ((6, 1), (0, 1), (7, 1), (1, 2), (3, 2), (5, 1))
SUMS = (
    (0, (0, 1)), (0, (6, 1)), (0, (1, 2)), (0, (7, 1)), (0, (3, 2)), (0, (5, 1)),
    (1, (0, 1)), (1, (6, 1)), (1, (1, 2)), (1, (7, 1)), (1, (3, 2)), (1, (5, 1)),
)
NORM = 1.0 / math.sqrt(NE - 1)


def rows_contract(a, b, precision=None):
    return lax.dot_general(
        a, b, (((1,), (1,)), ((), ())), precision=precision, preferred_element_type=F32
    )


def predict_kernel(
    prior_hbm, sens_hbm, pattern_hbm, own_hbm, obs_hbm, noise_hbm, pert_hbm,
    sys_ref, prior_all,
    pattern_ref, own_ref, obs_ref, noise_ref, pert_ref,
    sens_v, prior_v, prior_bf, t_buf, u_buf, pat_buf, owner, onehot, placed, x_in, x_own, z_in, z_all, first_sum,
    pred, pert_all, s_buf, d_buf, part, ab_in, c_in,
    load_sem, prior_sem, small_sem, own_sem, g_send, g_recv, u_send, u_recv, x_send, x_recv, z_send, z_recv,
    y_send, y_recv, r_send, r_recv,
):
    y, c, t = lax.axis_index("member"), lax.axis_index("slab"), lax.axis_index("tile")
    x, z = lax.div(t, NZ), lax.rem(t, NZ)

    def wrap(v, n):
        return lax.rem(v, n)

    def device(dy, dc, dx, dz):
        return (wrap(y + dy, NY), wrap(c + dc, NC), wrap(x + dx, NX) * NZ + wrap(z + dz, NZ))

    def send(src, dst, send_sem, recv_sem, to):
        pltpu.make_async_remote_copy(
            src_ref=src, dst_ref=dst, send_sem=send_sem, recv_sem=recv_sem,
            device_id=to, device_id_type=MESH,
        ).start()

    def wait(ref, sem):
        pltpu.make_async_copy(ref, ref, sem).wait()

    started = set()
    arrivals, ends = {}, []

    def expect(name, ref, send_sem, recv_sem):
        arrivals[name] = (ref, recv_sem)
        started.add(name)
        ends.append((ref, send_sem))

    def arrive(name):
        wait(*arrivals.pop(name))

    def finish():
        for name in list(arrivals):
            arrive(name)
        for pair in ends:
            wait(*pair)
        if "prior" in started:
            keep_prior.wait()

    load_prior = pltpu.make_async_copy(prior_hbm, prior_v, prior_sem)
    load_prior.start()
    loads = [
        pltpu.make_async_copy(sens_hbm.at[pl.ds(2 * i, 2)], sens_v.at[pl.ds(2 * i, 2)], load_sem.at[i])
        for i in range(NB // 2)
    ]
    small = [
        pltpu.make_async_copy(src, dst, small_sem.at[i])
        for i, (src, dst) in enumerate((
            (pattern_hbm, pattern_ref), (pert_hbm, pert_ref), (own_hbm, own_ref), (obs_hbm, obs_ref),
            (noise_hbm, noise_ref),
        ))
    ]
    small[0].start()
    for load in loads:
        load.start()
    for load in small[1:]:
        load.start()

    column = [(dy, dc, dx) for dy in range(NY) for dc in range(NC) for dx in range(NX)][1:]
    barrier = pltpu.get_barrier_semaphore()
    for dy, dc, dx in column:
        pl.semaphore_signal(barrier, inc=1, device_id=device(dy, dc, dx, 0), device_id_type=MESH)
    for dz in range(1, NZ):
        pl.semaphore_signal(barrier, inc=1, device_id=device(0, 0, 0, dz), device_id_type=MESH)

    small[0].wait()
    j = lax.broadcasted_iota(jnp.int32, (KB, 128), 1)
    k = lax.broadcasted_iota(jnp.int32, (KB, 128), 0)
    pick = (k == 2 * (j & 7) + ((j >> 4) & 1)).astype(F32)
    spread_rows = jnp.dot(pattern_ref[...].astype(F32), pick, precision=HIGHEST, preferred_element_type=F32)
    j = lax.broadcasted_iota(jnp.int32, (NB, 128), 1)
    b = lax.broadcasted_iota(jnp.int32, (NB, 128), 0)
    row = jnp.sum(
        jnp.where(b == 2 * (j >> 5) + ((j >> 3) & 1), spread_rows, 0.0), axis=0, keepdims=True
    )
    pat_buf[0] = jnp.broadcast_to(row, (8, 128))

    load_prior.wait()
    prior_bf[...] = prior_v[...].astype(BF16)
    low = lax.broadcasted_iota(jnp.int32, (16, 128), 1) < OB

    def slots(i):
        for r in range(MD // 2):
            ta = t_buf[pl.ds(i * 16 * MD + r, 16, stride=MD), :]
            tb = t_buf[pl.ds(i * 16 * MD + r + 16, 16, stride=MD), :]
            lanes = pl.ds(r % 2 * 128, 128)
            u_buf[r // 2, pl.ds(i * 32, 16), lanes] = jnp.where(low, ta, pltpu.roll(tb, OB, 1)).astype(BF16)
            u_buf[r // 2, pl.ds(i * 32 + 16, 16), lanes] = jnp.where(low, pltpu.roll(ta, OB, 1), tb).astype(BF16)

    def product(b):
        return rows_contract(prior_bf[:, b * PB : (b + 1) * PB], sens_v[b].reshape(KB * OB, PB))

    def keep(b, out):
        for kp in range(KB // 2):
            t_buf[pl.ds((b * 8 + kp) * MD, MD), :] = out[:, kp * 128 : (kp + 1) * 128]

    for i in range(NB // 2):
        loads[i].wait()
        out = product(2 * i)
        if i:
            slots(i - 1)
        keep(2 * i, out)
        keep(2 * i + 1, product(2 * i + 1))
    slots(NB // 2 - 1)

    for load in small[1:]:
        load.wait()
    for i in range(2):
        owned = own_ref[pl.ds(2 * c + i, 1), :].astype(F32)
        owned = jnp.broadcast_to(owned, (128, 128)).T
        owner[pl.ds(i * 128, 128), :] = owned
        onehot[pl.ds(i * 128, 128), pl.ds(0, 128)] = (owned == row).astype(F32).astype(BF16)
    pert_all[y] = pert_ref[...]

    pl.semaphore_wait(barrier, len(column) + NZ - 1)
    sibling = device(0, 1, 0, 0)
    send(pat_buf.at[0], pat_buf.at[1], u_send.at[NQ], u_recv.at[NQ], sibling)
    expect("pattern", pat_buf.at[1], u_send.at[NQ], u_recv.at[NQ])
    for group in PLACE:
        qs, at = pl.ds(*group), group[0]
        there = u_buf.at[qs, pl.ds(128, 128)]
        send(u_buf.at[qs, pl.ds(0, 128)], there, u_send.at[at], u_recv.at[at], sibling)
        expect(("u", group), there, u_send.at[at], u_recv.at[at])
    for dy in range(1, NY):
        send(pert_ref, pert_all.at[y], g_send.at[0], g_recv.at[0], device(dy, 0, 0, 0))
    expect("pert", pert_all.at[pl.ds(0, NY - 1)], g_send.at[0], g_recv.at[0])
    for dy in range(1, NY):
        send(prior_bf, prior_all.at[y], g_send.at[1], g_recv.at[1], device(dy, 0, 0, 0))
    expect("prior", prior_all.at[pl.ds(0, NY - 1)], g_send.at[1], g_recv.at[1])
    keep_prior = pltpu.make_async_copy(prior_bf, prior_all.at[y], own_sem)
    keep_prior.start()
    arrive("pattern")
    onehot[:, pl.ds(128, 128)] = (owner[...] == pat_buf[1, 0:1, :]).astype(F32).astype(BF16)

    def place(group):
        arrive(("u", group))
        for q in range(group[0], sum(group)):
            out = jnp.dot(onehot[...], u_buf[q], preferred_element_type=F32)
            out = jnp.concatenate(
                [out[:, :128].reshape(NX, NZ, 8, 128), out[:, 128:].reshape(NX, NZ, 8, 128)], axis=2
            )
            placed[q] = out.astype(BF16)

    x_land = {g: (x_in if g in X_FIRST else x_own) for g in X_FIRST + Z_FIRST}
    z_land = {g: (z_all if g in Z_FIRST else z_in) for g in X_FIRST + Z_FIRST}

    def send_x(group):
        qs, land = pl.ds(*group), x_land[group]
        for dx in range(1, NX):
            to = wrap(x + dx, NX)
            src = placed.at[qs, to] if group in X_FIRST else first_sum.at[qs, to]
            send(src, land.at[qs, dx - 1], x_send.at[group[0]], x_recv.at[group[0]], device(0, 0, dx, 0))
        expect(("x", group), land.at[qs], x_send.at[group[0]], x_recv.at[group[0]])

    def send_z(group):
        qs, land = pl.ds(*group), z_land[group]
        for dz in range(1, NZ):
            to = wrap(z + dz, NZ)
            src = placed.at[qs, :, to] if group in Z_FIRST else first_sum.at[qs, to]
            send(src, land.at[qs, dz - 1], z_send.at[group[0]], z_recv.at[group[0]], device(0, 0, 0, dz))
        expect(("z", group), land.at[qs], z_send.at[group[0]], z_recv.at[group[0]])

    def sum_first(group):
        if group in X_FIRST:
            arrive(("x", group))
            for q in range(group[0], sum(group)):
                total = placed[q, x].astype(F32)
                for d in range(NX - 1):
                    total += x_in[q, d].astype(F32)
                first_sum[q] = total.astype(BF16)
            send_z(group)
        else:
            arrive(("z", group))
            for q in range(group[0], sum(group)):
                total = placed[q, :, z].astype(F32)
                for d in range(NZ - 1):
                    total += z_all[q, d].astype(F32)
                first_sum[q, pl.ds(0, NX)] = total.astype(BF16)
            send_x(group)

    def sum_second(group):
        if group in X_FIRST:
            arrive(("z", group))
            parts, own = [z_in.at[:, d] for d in range(NZ - 1)], z
        else:
            arrive(("x", group))
            parts, own = [x_own.at[:, d] for d in range(NX - 1)], x
        for q in range(group[0], sum(group)):
            total = first_sum[q, own].astype(F32)
            for p in parts:
                total += p[q].astype(F32)
            pred[pl.ds(pl.multiple_of(y * 128 + q * 16, 16), 16), :] = total
        rows = pl.ds(pl.multiple_of(y * 128 + group[0] * 16, 16), group[1] * 16)
        for dy in range(1, NY):
            send(pred.at[rows], pred.at[rows], y_send.at[group[0]], y_recv.at[group[0]], device(dy, 0, 0, 0))
        expect(("y", group), pred.at[pl.ds(0, 48 * group[1])], y_send.at[group[0]], y_recv.at[group[0]])

    for group in PLACE:
        place(group)
        (send_x if group in X_FIRST else send_z)(group)

    for stage, group in SUMS:
        (sum_second if stage else sum_first)(group)
    arrive("pert")
    for group in X_FIRST + Z_FIRST:
        arrive(("y", group))

    low = lax.broadcasted_iota(jnp.int32, (NE // 2, 128), 1) < OB
    misfit = jnp.zeros((1, 1), F32)
    for n in range(OD // 128):
        even = pred[pl.ds(2 * n, NE // 2, stride=8), :]
        odd = pred[pl.ds(2 * n + 1, NE // 2, stride=8), :]
        first = jnp.where(low, even, pltpu.roll(odd, OB, 1))
        second = jnp.where(low, pltpu.roll(even, OB, 1), odd)
        pieces = []
        for w in range(NY):
            pieces += [first[w * 16 : (w + 1) * 16], second[w * 16 : (w + 1) * 16]]
        predicted = jnp.concatenate(pieces, axis=0)
        cols = pl.ds(n * 128, 128)
        noise = noise_ref[:, cols]
        mean = jnp.sum(predicted, axis=0, keepdims=True) / NE
        s_buf[:, cols] = (predicted - mean) * NORM / noise
        innovation = (obs_ref[:, cols] - predicted) / noise + pert_all[:, :, cols].reshape(NE, 128)
        d_buf[:, cols] = innovation
        misfit += jnp.sum(innovation * innovation, axis=(0, 1), keepdims=True)

    half = wrap(y, 2) * 64
    left = s_buf[pl.ds(pl.multiple_of(half, 64), 64), :]
    right = jnp.where(y < 2, s_buf[...], d_buf[...])
    quarter = rows_contract(left, right, HIGHEST)
    r_id = lax.broadcasted_iota(jnp.int32, (64, 128), 0) + half
    c_id = lax.broadcasted_iota(jnp.int32, (64, 128), 1)
    diagonal = jnp.logical_and(r_id == c_id, y < 2)
    quarter = quarter + jnp.where(diagonal, misfit / (4.0 * NE * NE), 0.0)
    part[...] = quarter.reshape(NC * NX, 8, 128)

    me = c * NX + x
    ab_in[me] = part[me]
    for dy, dc, dx in column:
        if dy == 0:
            to = wrap(c + dc, NC) * NX + wrap(x + dx, NX)
            send(part.at[to], ab_in.at[me], r_send.at[0], r_recv.at[0], device(0, dc, dx, 0))
    expect("ab", ab_in.at[pl.ds(0, NC * NX - 1)], r_send.at[0], r_recv.at[0])
    arrive("ab")
    total = ab_in[0]
    for n in range(1, NC * NX):
        total += ab_in[n]
    c_in[z] = total
    for dz in range(1, NZ):
        send(c_in.at[z], c_in.at[z], r_send.at[1], r_recv.at[1], device(0, 0, 0, dz))
    expect("c", c_in.at[pl.ds(0, NZ - 1)], r_send.at[1], r_recv.at[1])
    arrive("c")
    total = c_in[0]
    for n in range(1, NZ):
        total += c_in[n]
    rows = pl.ds(pl.multiple_of(y * 64 + me * 8, 8), 8)
    sys_ref[rows, :] = total
    for dy, dc, dx in column:
        send(sys_ref.at[rows], sys_ref.at[rows], r_send.at[2], r_recv.at[2], device(dy, dc, dx, 0))
    expect("rows", sys_ref.at[pl.ds(0, 8 * len(column))], r_send.at[2], r_recv.at[2])
    arrive("rows")

    finish()


def solve_kernel(
    sys_ref, prior_all, inc_hbm, weights_hbm, x_buf, w_buf, cen_buf, inc_buf, out_sem
):
    def mul(a, b):
        return jnp.dot(a, b, precision=HIGHEST, preferred_element_type=F32)

    def rough(a, b):
        return jnp.dot(a.astype(BF16), b.astype(BF16), preferred_element_type=F32)

    system, cross = sys_ref[:NE, :], sys_ref[NE:, :]
    eye = (
        lax.broadcasted_iota(jnp.int32, (NE, NE), 0) == lax.broadcasted_iota(jnp.int32, (NE, NE), 1)
    ).astype(F32)
    bound = jnp.max(jnp.sum(jnp.abs(system), axis=0, keepdims=True), axis=1, keepdims=True)
    start = eye / bound
    least = jnp.sum(jnp.sum(system, axis=0, keepdims=True), axis=1, keepdims=True) / NE
    inverse = eye * (2.0 / (bound + jnp.maximum(least, 0.0)))
    for _ in range(3):
        inverse = inverse + rough(inverse, eye - rough(system, inverse))
    weights = mul(inverse, cross)
    for _ in range(2):
        weights = weights + mul(inverse, cross - mul(system, weights))
    w_buf[...] = weights
    residual = cross - mul(system, weights)
    scale = jnp.sum(cross * cross)

    @pl.when(jnp.logical_not(jnp.sum(residual * residual) <= 1e-11 * scale))
    def _():
        x_buf[...] = start

        def step(carry):
            count, _ = carry
            inverse = x_buf[...]
            residual = eye - mul(sys_ref[:NE, :], inverse)
            x_buf[...] = inverse + mul(inverse, residual)
            return count + 1, jnp.sum(residual * residual)

        lax.while_loop(
            lambda carry: jnp.logical_and(carry[0] < 64, carry[1] > 1e-7), step, (0, jnp.float32(1.0))
        )
        w_buf[...] = mul(x_buf[...], sys_ref[NE:, :])
        for _ in range(2):
            residual = sys_ref[NE:, :] - mul(sys_ref[:NE, :], w_buf[...])
            w_buf[...] += mul(x_buf[...], residual)

    weights = w_buf[...]
    stores = [pltpu.make_async_copy(w_buf, weights_hbm, out_sem.at[4])]
    stores[0].start()
    centred = (weights - jnp.sum(weights, axis=0, keepdims=True) / NE) * NORM
    cen_buf[...] = centred.T
    y = lax.axis_index("member")
    own = cen_buf[pl.ds(pl.multiple_of(y * MD, MD), MD), :].astype(BF16)
    for n in range(4):
        cols = pl.ds(n * 1024, 1024)
        inc_buf[n] = jnp.dot(own, prior_all[:, :, cols].reshape(NE, 1024), preferred_element_type=F32)
        stores.append(pltpu.make_async_copy(inc_buf.at[n], inc_hbm.at[:, cols], out_sem.at[n]))
        stores[-1].start()
    for store in stores:
        store.wait()


def local(prior, sensitivity, pattern, ownership, observed, obs_noise, perturbation):
    vmem, anywhere = pl.BlockSpec(memory_space=pltpu.VMEM), pl.BlockSpec(memory_space=pl.ANY)
    hbm = pl.BlockSpec(memory_space=pltpu.HBM)
    dma = pltpu.SemaphoreType.DMA
    operands = [
        pltpu.with_memory_space_constraint(a, pltpu.HBM)
        for a in (
            prior, sensitivity, pattern, ownership.reshape(4, 128), observed.reshape(1, OD),
            obs_noise.reshape(1, OD), perturbation,
        )
    ]
    system, prior_all = pl.pallas_call(
        predict_kernel,
        out_shape=(
            jax.ShapeDtypeStruct((2 * NE, NE), F32),
            jax.ShapeDtypeStruct((NY, MD, PD), BF16),
        ),
        in_specs=[hbm] * 7,
        out_specs=(vmem, anywhere),
        scratch_shapes=[
            pltpu.VMEM((NB, KB), jnp.int32),
            pltpu.VMEM((4, 128), jnp.int32),
            pltpu.VMEM((1, OD), F32),
            pltpu.VMEM((1, OD), F32),
            pltpu.VMEM((MD, OD), F32),
            pltpu.VMEM((NB, KB, OB, PB), BF16),
            pltpu.VMEM((MD, PD), F32),
            pltpu.VMEM((MD, PD), BF16),
            pltpu.VMEM((NB * KB // 2 * MD, 128), F32),
            pltpu.VMEM((NQ, 256, 256), BF16),
            pltpu.VMEM((2, 8, 128), F32),
            pltpu.VMEM((256, 128), F32),
            pltpu.VMEM((256, 256), BF16),
            pltpu.VMEM((NQ, NX, NZ, 16, 128), BF16),
            pltpu.VMEM((NQ, NX - 1, NZ, 16, 128), BF16),
            pltpu.VMEM((NQ, NX - 1, 16, 128), BF16),
            pltpu.VMEM((NQ, NZ - 1, 16, 128), BF16),
            pltpu.VMEM((NQ, NZ - 1, NX, 16, 128), BF16),
            pltpu.VMEM((NQ, NZ, 16, 128), BF16),
            pltpu.VMEM((NY * 128, 128), F32),
            pltpu.VMEM((NY, MD, OD), F32),
            pltpu.VMEM((NE, OD), F32),
            pltpu.VMEM((NE, OD), F32),
            pltpu.VMEM((NC * NX, 8, 128), F32),
            pltpu.VMEM((NC * NX, 8, 128), F32),
            pltpu.VMEM((NZ, 8, 128), F32),
            dma((NB // 2,)), dma, dma((5,)), dma,
            dma((2,)), dma((2,)),
            dma((NQ + 1,)), dma((NQ + 1,)),
            dma((NQ,)), dma((NQ,)),
            dma((NQ,)), dma((NQ,)),
            dma((NQ,)), dma((NQ,)),
            dma((3,)), dma((3,)),
        ],
        compiler_params=pltpu.CompilerParams(
            collective_id=0, has_side_effects=True, vmem_limit_bytes=40 * 2**20
        ),
        name="predict",
    )(*operands)
    return pl.pallas_call(
        solve_kernel,
        out_shape=(
            jax.ShapeDtypeStruct((MD, PD), F32),
            jax.ShapeDtypeStruct((NE, NE), F32),
        ),
        in_specs=[vmem, vmem],
        out_specs=(anywhere, anywhere),
        scratch_shapes=[
            pltpu.VMEM((NE, NE), F32),
            pltpu.VMEM((NE, NE), F32),
            pltpu.VMEM((NE, NE), F32),
            pltpu.VMEM((4, MD, 1024), F32),
            dma((5,)),
        ],
        compiler_params=pltpu.CompilerParams(vmem_limit_bytes=24 * 2**20),
        name="solve",
    )(system, prior_all)


def solution(mesh):
    return jax.shard_map(
        local,
        mesh=mesh,
        in_specs=(
            P("member", ("slab", "tile")),
            P(("slab", "tile"), None, None, None),
            P(("slab", "tile"), None),
            P(),
            P(("slab", "tile")),
            P(("slab", "tile")),
            P("member", ("slab", "tile")),
        ),
        out_specs=(P("member", ("slab", "tile")), P()),
        check_vma=False,
    )
```

```python
import functools
import math

import jax
import jax.numpy as jnp
from jax import lax
from jax.experimental import pallas as pl
from jax.experimental.pallas import tpu as pltpu
from jax.sharding import PartitionSpec as P

MESH = pl.DeviceIdType.MESH
F32, BF16 = jnp.float32, jnp.bfloat16
HIGHEST = lax.Precision.HIGHEST

NY, NC, NX, NZ = 4, 2, 4, 8
MD = 32
NB, KB, OB, PB = 8, 16, 64, 512
PD = NB * PB
OD = 8 * OB
NE = NY * MD
NT = NX * NZ
NQ = 8
X_FIRST, Z_FIRST = ((0, 1), (1, 2), (3, 2), (5, 1)), ((6, 2),)
PLACE = ((0, 1), (6, 2), (1, 2), (3, 2), (5, 1))
SUMS = (
    (0, (0, 1)), (0, (1, 2)), (0, (6, 2)), (0, (3, 2)), (1, (0, 1)), (0, (5, 1)),
    (1, (1, 2)), (1, (6, 2)), (1, (3, 2)), (1, (5, 1)),
)
NORM = 1.0 / math.sqrt(NE - 1)


def rows_contract(a, b, precision=None):
    return lax.dot_general(
        a, b, (((1,), (1,)), ((), ())), precision=precision, preferred_element_type=F32
    )


def predict_kernel(
    prior_hbm, sens_hbm, pattern_hbm, own_hbm, obs_hbm, noise_hbm, pert_hbm,
    sys_ref, prior_all,
    pattern_ref, own_ref, obs_ref, noise_ref, pert_ref,
    sens_v, prior_v, prior_bf, t_buf, u_buf, pat_buf, owner, onehot, placed, x_in, x_own, z_in, z_all, first_sum,
    pred, pert_all, s_buf, d_buf, part, ab_in, c_in,
    load_sem, prior_sem, small_sem, own_sem, g_send, g_recv, u_send, u_recv, x_send, x_recv, z_send, z_recv,
    y_send, y_recv, r_send, r_recv,
):
    y, c, t = lax.axis_index("member"), lax.axis_index("slab"), lax.axis_index("tile")
    x, z = lax.div(t, NZ), lax.rem(t, NZ)

    def wrap(v, n):
        return lax.rem(v, n)

    def device(dy, dc, dx, dz):
        return (wrap(y + dy, NY), wrap(c + dc, NC), wrap(x + dx, NX) * NZ + wrap(z + dz, NZ))

    def send(src, dst, send_sem, recv_sem, to):
        pltpu.make_async_remote_copy(
            src_ref=src, dst_ref=dst, send_sem=send_sem, recv_sem=recv_sem,
            device_id=to, device_id_type=MESH,
        ).start()

    def wait(ref, sem):
        pltpu.make_async_copy(ref, ref, sem).wait()

    started = set()
    arrivals, ends = {}, []

    def expect(name, ref, send_sem, recv_sem):
        arrivals[name] = (ref, recv_sem)
        started.add(name)
        ends.append((ref, send_sem))

    def arrive(name):
        wait(*arrivals.pop(name))

    def finish():
        for name in list(arrivals):
            arrive(name)
        for pair in ends:
            wait(*pair)
        if "prior" in started:
            keep_prior.wait()

    load_prior = pltpu.make_async_copy(prior_hbm, prior_v, prior_sem)
    load_prior.start()
    loads = [
        pltpu.make_async_copy(sens_hbm.at[pl.ds(2 * i, 2)], sens_v.at[pl.ds(2 * i, 2)], load_sem.at[i])
        for i in range(NB // 2)
    ]
    small = [
        pltpu.make_async_copy(src, dst, small_sem.at[i])
        for i, (src, dst) in enumerate((
            (pattern_hbm, pattern_ref), (pert_hbm, pert_ref), (own_hbm, own_ref), (obs_hbm, obs_ref),
            (noise_hbm, noise_ref),
        ))
    ]
    small[0].start()
    for load in loads:
        load.start()
    for load in small[1:]:
        load.start()

    column = [(dy, dc, dx) for dy in range(NY) for dc in range(NC) for dx in range(NX)][1:]
    barrier = pltpu.get_barrier_semaphore()
    for dy, dc, dx in column:
        pl.semaphore_signal(barrier, inc=1, device_id=device(dy, dc, dx, 0), device_id_type=MESH)
    for dz in range(1, NZ):
        pl.semaphore_signal(barrier, inc=1, device_id=device(0, 0, 0, dz), device_id_type=MESH)

    small[0].wait()
    j = lax.broadcasted_iota(jnp.int32, (KB, 128), 1)
    k = lax.broadcasted_iota(jnp.int32, (KB, 128), 0)
    pick = (k == 2 * (j & 7) + ((j >> 4) & 1)).astype(F32)
    spread_rows = jnp.dot(pattern_ref[...].astype(F32), pick, precision=HIGHEST, preferred_element_type=F32)
    j = lax.broadcasted_iota(jnp.int32, (NB, 128), 1)
    b = lax.broadcasted_iota(jnp.int32, (NB, 128), 0)
    row = jnp.sum(
        jnp.where(b == 2 * (j >> 5) + ((j >> 3) & 1), spread_rows, 0.0), axis=0, keepdims=True
    )
    pat_buf[0] = jnp.broadcast_to(row, (8, 128))

    load_prior.wait()
    prior_bf[...] = prior_v[...].astype(BF16)
    low = lax.broadcasted_iota(jnp.int32, (16, 128), 1) < OB

    def slots(i):
        for r in range(MD // 2):
            ta = t_buf[pl.ds(i * 16 * MD + r, 16, stride=MD), :]
            tb = t_buf[pl.ds(i * 16 * MD + r + 16, 16, stride=MD), :]
            lanes = pl.ds(r % 2 * 128, 128)
            u_buf[r // 2, pl.ds(i * 32, 16), lanes] = jnp.where(low, ta, pltpu.roll(tb, OB, 1)).astype(BF16)
            u_buf[r // 2, pl.ds(i * 32 + 16, 16), lanes] = jnp.where(low, pltpu.roll(ta, OB, 1), tb).astype(BF16)

    def product(b):
        return rows_contract(prior_bf[:, b * PB : (b + 1) * PB], sens_v[b].reshape(KB * OB, PB))

    def keep(b, out):
        for kp in range(KB // 2):
            t_buf[pl.ds((b * 8 + kp) * MD, MD), :] = out[:, kp * 128 : (kp + 1) * 128]

    for i in range(NB // 2):
        loads[i].wait()
        out = product(2 * i)
        if i:
            slots(i - 1)
        keep(2 * i, out)
        keep(2 * i + 1, product(2 * i + 1))
    slots(NB // 2 - 1)

    for load in small[1:]:
        load.wait()
    for i in range(2):
        owned = own_ref[pl.ds(2 * c + i, 1), :].astype(F32)
        owned = jnp.broadcast_to(owned, (128, 128)).T
        owner[pl.ds(i * 128, 128), :] = owned
        onehot[pl.ds(i * 128, 128), pl.ds(0, 128)] = (owned == row).astype(F32).astype(BF16)
    pert_all[y] = pert_ref[...]

    pl.semaphore_wait(barrier, len(column) + NZ - 1)
    sibling = device(0, 1, 0, 0)
    send(pat_buf.at[0], pat_buf.at[1], u_send.at[NQ], u_recv.at[NQ], sibling)
    expect("pattern", pat_buf.at[1], u_send.at[NQ], u_recv.at[NQ])
    for group in PLACE:
        qs, at = pl.ds(*group), group[0]
        there = u_buf.at[qs, pl.ds(128, 128)]
        send(u_buf.at[qs, pl.ds(0, 128)], there, u_send.at[at], u_recv.at[at], sibling)
        expect(("u", group), there, u_send.at[at], u_recv.at[at])
    for dy in range(1, NY):
        send(pert_ref, pert_all.at[y], g_send.at[0], g_recv.at[0], device(dy, 0, 0, 0))
    expect("pert", pert_all.at[pl.ds(0, NY - 1)], g_send.at[0], g_recv.at[0])
    for dy in range(1, NY):
        send(prior_bf, prior_all.at[y], g_send.at[1], g_recv.at[1], device(dy, 0, 0, 0))
    expect("prior", prior_all.at[pl.ds(0, NY - 1)], g_send.at[1], g_recv.at[1])
    keep_prior = pltpu.make_async_copy(prior_bf, prior_all.at[y], own_sem)
    keep_prior.start()
    arrive("pattern")
    onehot[:, pl.ds(128, 128)] = (owner[...] == pat_buf[1, 0:1, :]).astype(F32).astype(BF16)

    def place(group):
        arrive(("u", group))
        for q in range(group[0], sum(group)):
            out = jnp.dot(onehot[...], u_buf[q], preferred_element_type=F32)
            out = jnp.concatenate(
                [out[:, :128].reshape(NX, NZ, 8, 128), out[:, 128:].reshape(NX, NZ, 8, 128)], axis=2
            )
            placed[q] = out.astype(BF16)

    x_land = {g: (x_in if g in X_FIRST else x_own) for g in X_FIRST + Z_FIRST}
    z_land = {g: (z_all if g in Z_FIRST else z_in) for g in X_FIRST + Z_FIRST}

    def send_x(group):
        qs, land = pl.ds(*group), x_land[group]
        for dx in range(1, NX):
            to = wrap(x + dx, NX)
            src = placed.at[qs, to] if group in X_FIRST else first_sum.at[qs, to]
            send(src, land.at[qs, dx - 1], x_send.at[group[0]], x_recv.at[group[0]], device(0, 0, dx, 0))
        expect(("x", group), land.at[qs], x_send.at[group[0]], x_recv.at[group[0]])

    def send_z(group):
        qs, land = pl.ds(*group), z_land[group]
        for dz in range(1, NZ):
            to = wrap(z + dz, NZ)
            src = placed.at[qs, :, to] if group in Z_FIRST else first_sum.at[qs, to]
            send(src, land.at[qs, dz - 1], z_send.at[group[0]], z_recv.at[group[0]], device(0, 0, 0, dz))
        expect(("z", group), land.at[qs], z_send.at[group[0]], z_recv.at[group[0]])

    def sum_first(group):
        if group in X_FIRST:
            arrive(("x", group))
            for q in range(group[0], sum(group)):
                total = placed[q, x].astype(F32)
                for d in range(NX - 1):
                    total += x_in[q, d].astype(F32)
                first_sum[q] = total.astype(BF16)
            send_z(group)
        else:
            arrive(("z", group))
            for q in range(group[0], sum(group)):
                total = placed[q, :, z].astype(F32)
                for d in range(NZ - 1):
                    total += z_all[q, d].astype(F32)
                first_sum[q, pl.ds(0, NX)] = total.astype(BF16)
            send_x(group)

    def sum_second(group):
        if group in X_FIRST:
            arrive(("z", group))
            parts, own = [z_in.at[:, d] for d in range(NZ - 1)], z
        else:
            arrive(("x", group))
            parts, own = [x_own.at[:, d] for d in range(NX - 1)], x
        for q in range(group[0], sum(group)):
            total = first_sum[q, own].astype(F32)
            for p in parts:
                total += p[q].astype(F32)
            pred[pl.ds(pl.multiple_of(y * 128 + q * 16, 16), 16), :] = total
        rows = pl.ds(pl.multiple_of(y * 128 + group[0] * 16, 16), group[1] * 16)
        for dy in range(1, NY):
            send(pred.at[rows], pred.at[rows], y_send.at[group[0]], y_recv.at[group[0]], device(dy, 0, 0, 0))
        expect(("y", group), pred.at[pl.ds(0, 48 * group[1])], y_send.at[group[0]], y_recv.at[group[0]])

    for group in PLACE:
        place(group)
        (send_x if group in X_FIRST else send_z)(group)

    for stage, group in SUMS:
        (sum_second if stage else sum_first)(group)
    arrive("pert")
    for group in X_FIRST + Z_FIRST:
        arrive(("y", group))

    low = lax.broadcasted_iota(jnp.int32, (NE // 2, 128), 1) < OB
    misfit = jnp.zeros((1, 1), F32)
    for n in range(OD // 128):
        even = pred[pl.ds(2 * n, NE // 2, stride=8), :]
        odd = pred[pl.ds(2 * n + 1, NE // 2, stride=8), :]
        first = jnp.where(low, even, pltpu.roll(odd, OB, 1))
        second = jnp.where(low, pltpu.roll(even, OB, 1), odd)
        pieces = []
        for w in range(NY):
            pieces += [first[w * 16 : (w + 1) * 16], second[w * 16 : (w + 1) * 16]]
        predicted = jnp.concatenate(pieces, axis=0)
        cols = pl.ds(n * 128, 128)
        noise = noise_ref[:, cols]
        mean = jnp.sum(predicted, axis=0, keepdims=True) / NE
        s_buf[:, cols] = (predicted - mean) * NORM / noise
        innovation = (obs_ref[:, cols] - predicted) / noise + pert_all[:, :, cols].reshape(NE, 128)
        d_buf[:, cols] = innovation
        misfit += jnp.sum(innovation * innovation, axis=(0, 1), keepdims=True)

    half = wrap(y, 2) * 64
    left = s_buf[pl.ds(pl.multiple_of(half, 64), 64), :]
    right = jnp.where(y < 2, s_buf[...], d_buf[...])
    quarter = rows_contract(left, right, HIGHEST)
    r_id = lax.broadcasted_iota(jnp.int32, (64, 128), 0) + half
    c_id = lax.broadcasted_iota(jnp.int32, (64, 128), 1)
    diagonal = jnp.logical_and(r_id == c_id, y < 2)
    quarter = quarter + jnp.where(diagonal, misfit / (4.0 * NE * NE), 0.0)
    part[...] = quarter.reshape(NC * NX, 8, 128)

    me = c * NX + x
    ab_in[me] = part[me]
    for dy, dc, dx in column:
        if dy == 0:
            to = wrap(c + dc, NC) * NX + wrap(x + dx, NX)
            send(part.at[to], ab_in.at[me], r_send.at[0], r_recv.at[0], device(0, dc, dx, 0))
    expect("ab", ab_in.at[pl.ds(0, NC * NX - 1)], r_send.at[0], r_recv.at[0])
    arrive("ab")
    total = ab_in[0]
    for n in range(1, NC * NX):
        total += ab_in[n]
    c_in[z] = total
    for dz in range(1, NZ):
        send(c_in.at[z], c_in.at[z], r_send.at[1], r_recv.at[1], device(0, 0, 0, dz))
    expect("c", c_in.at[pl.ds(0, NZ - 1)], r_send.at[1], r_recv.at[1])
    arrive("c")
    total = c_in[0]
    for n in range(1, NZ):
        total += c_in[n]
    rows = pl.ds(pl.multiple_of(y * 64 + me * 8, 8), 8)
    sys_ref[rows, :] = total
    for dy, dc, dx in column:
        send(sys_ref.at[rows], sys_ref.at[rows], r_send.at[2], r_recv.at[2], device(dy, dc, dx, 0))
    expect("rows", sys_ref.at[pl.ds(0, 8 * len(column))], r_send.at[2], r_recv.at[2])
    arrive("rows")

    finish()


def solve_kernel(
    sys_ref, prior_all, inc_hbm, weights_hbm, x_buf, w_buf, cen_buf, inc_buf, out_sem
):
    def mul(a, b):
        return jnp.dot(a, b, precision=HIGHEST, preferred_element_type=F32)

    def rough(a, b):
        return jnp.dot(a.astype(BF16), b.astype(BF16), preferred_element_type=F32)

    system, cross = sys_ref[:NE, :], sys_ref[NE:, :]
    eye = (
        lax.broadcasted_iota(jnp.int32, (NE, NE), 0) == lax.broadcasted_iota(jnp.int32, (NE, NE), 1)
    ).astype(F32)
    bound = jnp.max(jnp.sum(jnp.abs(system), axis=0, keepdims=True), axis=1, keepdims=True)
    start = eye / bound
    least = jnp.sum(jnp.sum(system, axis=0, keepdims=True), axis=1, keepdims=True) / NE
    inverse = eye * (2.0 / (bound + jnp.maximum(least, 0.0)))
    for _ in range(3):
        inverse = inverse + rough(inverse, eye - rough(system, inverse))
    weights = rough(inverse, cross)
    for _ in range(2):
        weights = weights + rough(inverse, cross - mul(system, weights))
    residual = cross - mul(system, weights)
    y = lax.axis_index("member")

    def update(weights):
        w_buf[...] = weights
        centred = (weights - jnp.sum(weights, axis=0, keepdims=True) / NE) * NORM
        cen_buf[...] = centred.T
        own = cen_buf[pl.ds(pl.multiple_of(y * MD, MD), MD), :].astype(BF16)
        for n in range(4):
            cols = pl.ds(n * 1024, 1024)
            inc_buf[n] = jnp.dot(own, prior_all[:, :, cols].reshape(NE, 1024), preferred_element_type=F32)

    update(weights)

    @pl.when(jnp.logical_not(jnp.sum(residual * residual) <= 1e-10 * jnp.sum(cross * cross)))
    def _():
        x_buf[...] = start

        def step(carry):
            count, _ = carry
            inverse = x_buf[...]
            residual = eye - mul(sys_ref[:NE, :], inverse)
            x_buf[...] = inverse + mul(inverse, residual)
            return count + 1, jnp.sum(residual * residual)

        lax.while_loop(
            lambda carry: jnp.logical_and(carry[0] < 64, carry[1] > 1e-7), step, (0, jnp.float32(1.0))
        )
        weights = mul(x_buf[...], sys_ref[NE:, :])
        for _ in range(2):
            weights = weights + mul(x_buf[...], sys_ref[NE:, :] - mul(sys_ref[:NE, :], weights))
        update(weights)

    stores = [pltpu.make_async_copy(w_buf, weights_hbm, out_sem.at[4])]
    for n in range(4):
        stores.append(pltpu.make_async_copy(inc_buf.at[n], inc_hbm.at[:, pl.ds(n * 1024, 1024)], out_sem.at[n]))
    for store in stores:
        store.start()
    for store in stores:
        store.wait()


def local(prior, sensitivity, pattern, ownership, observed, obs_noise, perturbation):
    vmem, anywhere = pl.BlockSpec(memory_space=pltpu.VMEM), pl.BlockSpec(memory_space=pl.ANY)
    hbm = pl.BlockSpec(memory_space=pltpu.HBM)
    dma = pltpu.SemaphoreType.DMA
    operands = [
        pltpu.with_memory_space_constraint(a, pltpu.HBM)
        for a in (
            prior, sensitivity, pattern, ownership.reshape(4, 128), observed.reshape(1, OD),
            obs_noise.reshape(1, OD), perturbation,
        )
    ]
    system, prior_all = pl.pallas_call(
        predict_kernel,
        out_shape=(
            jax.ShapeDtypeStruct((2 * NE, NE), F32),
            jax.ShapeDtypeStruct((NY, MD, PD), BF16),
        ),
        in_specs=[hbm] * 7,
        out_specs=(vmem, anywhere),
        scratch_shapes=[
            pltpu.VMEM((NB, KB), jnp.int32),
            pltpu.VMEM((4, 128), jnp.int32),
            pltpu.VMEM((1, OD), F32),
            pltpu.VMEM((1, OD), F32),
            pltpu.VMEM((MD, OD), F32),
            pltpu.VMEM((NB, KB, OB, PB), BF16),
            pltpu.VMEM((MD, PD), F32),
            pltpu.VMEM((MD, PD), BF16),
            pltpu.VMEM((NB * KB // 2 * MD, 128), F32),
            pltpu.VMEM((NQ, 256, 256), BF16),
            pltpu.VMEM((2, 8, 128), F32),
            pltpu.VMEM((256, 128), F32),
            pltpu.VMEM((256, 256), BF16),
            pltpu.VMEM((NQ, NX, NZ, 16, 128), BF16),
            pltpu.VMEM((NQ, NX - 1, NZ, 16, 128), BF16),
            pltpu.VMEM((NQ, NX - 1, 16, 128), BF16),
            pltpu.VMEM((NQ, NZ - 1, 16, 128), BF16),
            pltpu.VMEM((NQ, NZ - 1, NX, 16, 128), BF16),
            pltpu.VMEM((NQ, NZ, 16, 128), BF16),
            pltpu.VMEM((NY * 128, 128), F32),
            pltpu.VMEM((NY, MD, OD), F32),
            pltpu.VMEM((NE, OD), F32),
            pltpu.VMEM((NE, OD), F32),
            pltpu.VMEM((NC * NX, 8, 128), F32),
            pltpu.VMEM((NC * NX, 8, 128), F32),
            pltpu.VMEM((NZ, 8, 128), F32),
            dma((NB // 2,)), dma, dma((5,)), dma,
            dma((2,)), dma((2,)),
            dma((NQ + 1,)), dma((NQ + 1,)),
            dma((NQ,)), dma((NQ,)),
            dma((NQ,)), dma((NQ,)),
            dma((NQ,)), dma((NQ,)),
            dma((3,)), dma((3,)),
        ],
        compiler_params=pltpu.CompilerParams(
            collective_id=0, has_side_effects=True, vmem_limit_bytes=40 * 2**20
        ),
        name="predict",
    )(*operands)
    return pl.pallas_call(
        solve_kernel,
        out_shape=(
            jax.ShapeDtypeStruct((MD, PD), F32),
            jax.ShapeDtypeStruct((NE, NE), F32),
        ),
        in_specs=[vmem, vmem],
        out_specs=(anywhere, anywhere),
        scratch_shapes=[
            pltpu.VMEM((NE, NE), F32),
            pltpu.VMEM((NE, NE), F32),
            pltpu.VMEM((NE, NE), F32),
            pltpu.VMEM((4, MD, 1024), F32),
            dma((5,)),
        ],
        compiler_params=pltpu.CompilerParams(vmem_limit_bytes=24 * 2**20),
        name="solve",
    )(system, prior_all)


def solution(mesh):
    return jax.shard_map(
        local,
        mesh=mesh,
        in_specs=(
            P("member", ("slab", "tile")),
            P(("slab", "tile"), None, None, None),
            P(("slab", "tile"), None),
            P(),
            P(("slab", "tile")),
            P(("slab", "tile")),
            P("member", ("slab", "tile")),
        ),
        out_specs=(P("member", ("slab", "tile")), P()),
        check_vma=False,
    )
```

```python
import functools
import math

import jax
import jax.numpy as jnp
from jax import lax
from jax.experimental import pallas as pl
from jax.experimental.pallas import tpu as pltpu
from jax.sharding import PartitionSpec as P

MESH = pl.DeviceIdType.MESH
F32, BF16 = jnp.float32, jnp.bfloat16
HIGHEST = lax.Precision.HIGHEST

NY, NC, NX, NZ = 4, 2, 4, 8
MD = 32
NB, KB, OB, PB = 8, 16, 64, 512
PD = NB * PB
OD = 8 * OB
NE = NY * MD
NT = NX * NZ
NQ = 8
X_FIRST, Z_FIRST = ((0, 1), (1, 2), (3, 2), (5, 1)), ((6, 2),)
PLACE = ((0, 1), (6, 2), (1, 2), (3, 2), (5, 1))
SUMS = (
    (0, (0, 1)), (0, (1, 2)), (0, (6, 2)), (0, (3, 2)), (1, (0, 1)), (0, (5, 1)),
    (1, (1, 2)), (1, (6, 2)), (1, (3, 2)), (1, (5, 1)),
)
NORM = 1.0 / math.sqrt(NE - 1)


def rows_contract(a, b, precision=None):
    return lax.dot_general(
        a, b, (((1,), (1,)), ((), ())), precision=precision, preferred_element_type=F32
    )


def predict_kernel(
    prior_hbm, sens_hbm, pattern_hbm, own_hbm, obs_hbm, noise_hbm, pert_hbm,
    sys_ref, prior_all,
    pattern_ref, own_ref, obs_ref, noise_ref, pert_ref,
    sens_v, prior_v, prior_bf, t_buf, u_buf, pat_buf, owner, onehot, placed, x_in, x_own, z_in, z_all, first_sum,
    pred, pert_all, s_buf, d_buf, part, ab_in, c_in,
    load_sem, prior_sem, small_sem, own_sem, g_send, g_recv, u_send, u_recv, x_send, x_recv, z_send, z_recv,
    y_send, y_recv, r_send, r_recv,
):
    y, c, t = lax.axis_index("member"), lax.axis_index("slab"), lax.axis_index("tile")
    x, z = lax.div(t, NZ), lax.rem(t, NZ)

    def wrap(v, n):
        return lax.rem(v, n)

    def device(dy, dc, dx, dz):
        return (wrap(y + dy, NY), wrap(c + dc, NC), wrap(x + dx, NX) * NZ + wrap(z + dz, NZ))

    def send(src, dst, send_sem, recv_sem, to):
        pltpu.make_async_remote_copy(
            src_ref=src, dst_ref=dst, send_sem=send_sem, recv_sem=recv_sem,
            device_id=to, device_id_type=MESH,
        ).start()

    def wait(ref, sem):
        pltpu.make_async_copy(ref, ref, sem).wait()

    started = set()
    arrivals, ends = {}, []

    def expect(name, ref, send_sem, recv_sem):
        arrivals[name] = (ref, recv_sem)
        started.add(name)
        ends.append((ref, send_sem))

    def arrive(name):
        wait(*arrivals.pop(name))

    def finish():
        for name in list(arrivals):
            arrive(name)
        while ends:
            wait(*ends.pop())
        if "prior" in started:
            keep_prior.wait()

    load_prior = pltpu.make_async_copy(prior_hbm, prior_v, prior_sem)
    load_prior.start()
    loads = [
        pltpu.make_async_copy(sens_hbm.at[pl.ds(2 * i, 2)], sens_v.at[pl.ds(2 * i, 2)], load_sem.at[i])
        for i in range(NB // 2)
    ]
    small = [
        pltpu.make_async_copy(src, dst, small_sem.at[i])
        for i, (src, dst) in enumerate((
            (pattern_hbm, pattern_ref), (pert_hbm, pert_ref), (own_hbm, own_ref), (obs_hbm, obs_ref),
            (noise_hbm, noise_ref),
        ))
    ]
    small[0].start()
    for load in loads:
        load.start()
    for load in small[1:]:
        load.start()

    column = [(dy, dc, dx) for dy in range(NY) for dc in range(NC) for dx in range(NX)][1:]
    barrier = pltpu.get_barrier_semaphore()
    for dy, dc, dx in column:
        pl.semaphore_signal(barrier, inc=1, device_id=device(dy, dc, dx, 0), device_id_type=MESH)
    for dz in range(1, NZ):
        pl.semaphore_signal(barrier, inc=1, device_id=device(0, 0, 0, dz), device_id_type=MESH)

    small[0].wait()
    j = lax.broadcasted_iota(jnp.int32, (KB, 128), 1)
    k = lax.broadcasted_iota(jnp.int32, (KB, 128), 0)
    pick = (k == 2 * (j & 7) + ((j >> 4) & 1)).astype(F32)
    spread_rows = jnp.dot(pattern_ref[...].astype(F32), pick, precision=HIGHEST, preferred_element_type=F32)
    j = lax.broadcasted_iota(jnp.int32, (NB, 128), 1)
    b = lax.broadcasted_iota(jnp.int32, (NB, 128), 0)
    row = jnp.sum(
        jnp.where(b == 2 * (j >> 5) + ((j >> 3) & 1), spread_rows, 0.0), axis=0, keepdims=True
    )
    pat_buf[0] = jnp.broadcast_to(row, (8, 128))

    load_prior.wait()
    prior_bf[...] = prior_v[...].astype(BF16)
    low = lax.broadcasted_iota(jnp.int32, (16, 128), 1) < OB

    def slots(i):
        for r in range(MD // 2):
            ta = t_buf[pl.ds(i * 16 * MD + r, 16, stride=MD), :]
            tb = t_buf[pl.ds(i * 16 * MD + r + 16, 16, stride=MD), :]
            lanes = pl.ds(r % 2 * 128, 128)
            u_buf[r // 2, pl.ds(i * 32, 16), lanes] = jnp.where(low, ta, pltpu.roll(tb, OB, 1)).astype(BF16)
            u_buf[r // 2, pl.ds(i * 32 + 16, 16), lanes] = jnp.where(low, pltpu.roll(ta, OB, 1), tb).astype(BF16)

    def product(b):
        return rows_contract(prior_bf[:, b * PB : (b + 1) * PB], sens_v[b].reshape(KB * OB, PB))

    def keep(b, out):
        for kp in range(KB // 2):
            t_buf[pl.ds((b * 8 + kp) * MD, MD), :] = out[:, kp * 128 : (kp + 1) * 128]

    for i in range(NB // 2):
        loads[i].wait()
        out = product(2 * i)
        if i:
            slots(i - 1)
        keep(2 * i, out)
        keep(2 * i + 1, product(2 * i + 1))
    slots(NB // 2 - 1)

    for load in small[1:]:
        load.wait()
    for i in range(2):
        owned = own_ref[pl.ds(2 * c + i, 1), :].astype(F32)
        owned = jnp.broadcast_to(owned, (128, 128)).T
        owner[pl.ds(i * 128, 128), :] = owned
        onehot[pl.ds(i * 128, 128), pl.ds(0, 128)] = (owned == row).astype(F32).astype(BF16)
    pert_all[y] = pert_ref[...]

    pl.semaphore_wait(barrier, len(column) + NZ - 1)
    sibling = device(0, 1, 0, 0)
    send(pat_buf.at[0], pat_buf.at[1], u_send.at[NQ], u_recv.at[NQ], sibling)
    expect("pattern", pat_buf.at[1], u_send.at[NQ], u_recv.at[NQ])
    for group in PLACE:
        qs, at = pl.ds(*group), group[0]
        there = u_buf.at[qs, pl.ds(128, 128)]
        send(u_buf.at[qs, pl.ds(0, 128)], there, u_send.at[at], u_recv.at[at], sibling)
        expect(("u", group), there, u_send.at[at], u_recv.at[at])
    for dy in range(1, NY):
        send(pert_ref, pert_all.at[y], g_send.at[0], g_recv.at[0], device(dy, 0, 0, 0))
    expect("pert", pert_all.at[pl.ds(0, NY - 1)], g_send.at[0], g_recv.at[0])
    for dy in range(1, NY):
        send(prior_bf, prior_all.at[y], g_send.at[1], g_recv.at[1], device(dy, 0, 0, 0))
    expect("prior", prior_all.at[pl.ds(0, NY - 1)], g_send.at[1], g_recv.at[1])
    keep_prior = pltpu.make_async_copy(prior_bf, prior_all.at[y], own_sem)
    keep_prior.start()
    arrive("pattern")
    onehot[:, pl.ds(128, 128)] = (owner[...] == pat_buf[1, 0:1, :]).astype(F32).astype(BF16)

    def place(group):
        arrive(("u", group))
        for q in range(group[0], sum(group)):
            out = jnp.dot(onehot[...], u_buf[q], preferred_element_type=F32)
            out = jnp.concatenate(
                [out[:, :128].reshape(NX, NZ, 8, 128), out[:, 128:].reshape(NX, NZ, 8, 128)], axis=2
            )
            placed[q] = out.astype(BF16)

    x_land = {g: (x_in if g in X_FIRST else x_own) for g in X_FIRST + Z_FIRST}
    z_land = {g: (z_all if g in Z_FIRST else z_in) for g in X_FIRST + Z_FIRST}

    def send_x(group):
        qs, land = pl.ds(*group), x_land[group]
        for dx in range(1, NX):
            to = wrap(x + dx, NX)
            src = placed.at[qs, to] if group in X_FIRST else first_sum.at[qs, to]
            send(src, land.at[qs, dx - 1], x_send.at[group[0]], x_recv.at[group[0]], device(0, 0, dx, 0))
        expect(("x", group), land.at[qs], x_send.at[group[0]], x_recv.at[group[0]])

    def send_z(group):
        qs, land = pl.ds(*group), z_land[group]
        for dz in range(1, NZ):
            to = wrap(z + dz, NZ)
            src = placed.at[qs, :, to] if group in Z_FIRST else first_sum.at[qs, to]
            send(src, land.at[qs, dz - 1], z_send.at[group[0]], z_recv.at[group[0]], device(0, 0, 0, dz))
        expect(("z", group), land.at[qs], z_send.at[group[0]], z_recv.at[group[0]])

    def sum_first(group):
        if group in X_FIRST:
            arrive(("x", group))
            for q in range(group[0], sum(group)):
                total = placed[q, x].astype(F32)
                for d in range(NX - 1):
                    total += x_in[q, d].astype(F32)
                first_sum[q] = total.astype(BF16)
            send_z(group)
        else:
            arrive(("z", group))
            for q in range(group[0], sum(group)):
                total = placed[q, :, z].astype(F32)
                for d in range(NZ - 1):
                    total += z_all[q, d].astype(F32)
                first_sum[q, pl.ds(0, NX)] = total.astype(BF16)
            send_x(group)

    def sum_second(group):
        if group in X_FIRST:
            arrive(("z", group))
            parts, own = [z_in.at[:, d] for d in range(NZ - 1)], z
        else:
            arrive(("x", group))
            parts, own = [x_own.at[:, d] for d in range(NX - 1)], x
        for q in range(group[0], sum(group)):
            total = first_sum[q, own].astype(F32)
            for p in parts:
                total += p[q].astype(F32)
            pred[pl.ds(pl.multiple_of(y * 128 + q * 16, 16), 16), :] = total
        rows = pl.ds(pl.multiple_of(y * 128 + group[0] * 16, 16), group[1] * 16)
        for dy in range(1, NY):
            send(pred.at[rows], pred.at[rows], y_send.at[group[0]], y_recv.at[group[0]], device(dy, 0, 0, 0))
        expect(("y", group), pred.at[pl.ds(0, 48 * group[1])], y_send.at[group[0]], y_recv.at[group[0]])

    for group in PLACE:
        place(group)
        (send_x if group in X_FIRST else send_z)(group)

    for stage, group in SUMS:
        (sum_second if stage else sum_first)(group)
    arrive("pert")
    for group in X_FIRST + Z_FIRST:
        arrive(("y", group))

    low = lax.broadcasted_iota(jnp.int32, (NE // 2, 128), 1) < OB
    misfit = jnp.zeros((1, 1), F32)
    for n in range(OD // 128):
        even = pred[pl.ds(2 * n, NE // 2, stride=8), :]
        odd = pred[pl.ds(2 * n + 1, NE // 2, stride=8), :]
        first = jnp.where(low, even, pltpu.roll(odd, OB, 1))
        second = jnp.where(low, pltpu.roll(even, OB, 1), odd)
        pieces = []
        for w in range(NY):
            pieces += [first[w * 16 : (w + 1) * 16], second[w * 16 : (w + 1) * 16]]
        predicted = jnp.concatenate(pieces, axis=0)
        cols = pl.ds(n * 128, 128)
        noise = noise_ref[:, cols]
        mean = jnp.sum(predicted, axis=0, keepdims=True) / NE
        s_buf[:, cols] = (predicted - mean) * NORM / noise
        innovation = (obs_ref[:, cols] - predicted) / noise + pert_all[:, :, cols].reshape(NE, 128)
        d_buf[:, cols] = innovation
        misfit += jnp.sum(innovation * innovation, axis=(0, 1), keepdims=True)

    half = wrap(y, 2) * 64
    left = s_buf[pl.ds(pl.multiple_of(half, 64), 64), :]
    right = jnp.where(y < 2, s_buf[...], d_buf[...])
    quarter = rows_contract(left, right, HIGHEST)
    r_id = lax.broadcasted_iota(jnp.int32, (64, 128), 0) + half
    c_id = lax.broadcasted_iota(jnp.int32, (64, 128), 1)
    diagonal = jnp.logical_and(r_id == c_id, y < 2)
    quarter = quarter + jnp.where(diagonal, misfit / (4.0 * NE * NE), 0.0)
    part[...] = quarter.reshape(NC * NX, 8, 128)

    me = c * NX + x
    ab_in[me] = part[me]
    for dy, dc, dx in column:
        if dy == 0:
            to = wrap(c + dc, NC) * NX + wrap(x + dx, NX)
            send(part.at[to], ab_in.at[me], r_send.at[0], r_recv.at[0], device(0, dc, dx, 0))
    expect("ab", ab_in.at[pl.ds(0, NC * NX - 1)], r_send.at[0], r_recv.at[0])
    arrive("ab")
    total = ab_in[0]
    for n in range(1, NC * NX):
        total += ab_in[n]
    c_in[z] = total
    for dz in range(1, NZ):
        send(c_in.at[z], c_in.at[z], r_send.at[1], r_recv.at[1], device(0, 0, 0, dz))
    expect("c", c_in.at[pl.ds(0, NZ - 1)], r_send.at[1], r_recv.at[1])
    arrive("c")
    total = c_in[0]
    for n in range(1, NZ):
        total += c_in[n]
    rows = pl.ds(pl.multiple_of(y * 64 + me * 8, 8), 8)
    sys_ref[rows, :] = total
    for dy, dc, dx in column:
        send(sys_ref.at[rows], sys_ref.at[rows], r_send.at[2], r_recv.at[2], device(dy, dc, dx, 0))
    finish()
    expect("rows", sys_ref.at[pl.ds(0, 8 * len(column))], r_send.at[2], r_recv.at[2])
    arrive("rows")
    wait(*ends.pop())


def solve_kernel(
    sys_ref, prior_all, inc_hbm, weights_hbm, x_buf, w_buf, cen_buf, inc_buf, out_sem
):
    def mul(a, b):
        return jnp.dot(a, b, precision=HIGHEST, preferred_element_type=F32)

    def rough(a, b):
        return jnp.dot(a.astype(BF16), b.astype(BF16), preferred_element_type=F32)

    system, cross = sys_ref[:NE, :], sys_ref[NE:, :]
    eye = (
        lax.broadcasted_iota(jnp.int32, (NE, NE), 0) == lax.broadcasted_iota(jnp.int32, (NE, NE), 1)
    ).astype(F32)
    size = jnp.sum(jnp.abs(system), axis=0, keepdims=True)
    inverse = eye * (2.0 / (size + jnp.maximum(jnp.sum(system, axis=0, keepdims=True), 0.0)))
    for _ in range(2):
        inverse = inverse + rough(inverse, eye - rough(system, inverse))
    weights = rough(inverse, cross)
    for _ in range(2):
        weights = weights + rough(inverse, cross - mul(system, weights))
    residual = cross - mul(system, weights)
    y = lax.axis_index("member")

    def update(weights):
        w_buf[...] = weights
        centred = (weights - jnp.sum(weights, axis=0, keepdims=True) / NE) * NORM
        cen_buf[...] = centred.T
        own = cen_buf[pl.ds(pl.multiple_of(y * MD, MD), MD), :].astype(BF16)
        for n in range(4):
            cols = pl.ds(n * 1024, 1024)
            inc_buf[n] = jnp.dot(own, prior_all[:, :, cols].reshape(NE, 1024), preferred_element_type=F32)

    update(weights)

    @pl.when(jnp.logical_not(jnp.sum(residual * residual) <= 1e-10 * jnp.sum(cross * cross)))
    def _():
        x_buf[...] = eye / jnp.max(size, axis=1, keepdims=True)

        def step(carry):
            count, _ = carry
            inverse = x_buf[...]
            residual = eye - mul(sys_ref[:NE, :], inverse)
            x_buf[...] = inverse + mul(inverse, residual)
            return count + 1, jnp.sum(residual * residual)

        lax.while_loop(
            lambda carry: jnp.logical_and(carry[0] < 64, carry[1] > 1e-7), step, (0, jnp.float32(1.0))
        )
        weights = mul(x_buf[...], sys_ref[NE:, :])
        for _ in range(2):
            weights = weights + mul(x_buf[...], sys_ref[NE:, :] - mul(sys_ref[:NE, :], weights))
        update(weights)

    stores = [pltpu.make_async_copy(w_buf, weights_hbm, out_sem.at[4])]
    for n in range(4):
        stores.append(pltpu.make_async_copy(inc_buf.at[n], inc_hbm.at[:, pl.ds(n * 1024, 1024)], out_sem.at[n]))
    for store in stores:
        store.start()
    for store in stores:
        store.wait()


def local(prior, sensitivity, pattern, ownership, observed, obs_noise, perturbation):
    vmem, anywhere = pl.BlockSpec(memory_space=pltpu.VMEM), pl.BlockSpec(memory_space=pl.ANY)
    hbm = pl.BlockSpec(memory_space=pltpu.HBM)
    dma = pltpu.SemaphoreType.DMA
    operands = [
        pltpu.with_memory_space_constraint(a, pltpu.HBM)
        for a in (
            prior, sensitivity, pattern, ownership.reshape(4, 128), observed.reshape(1, OD),
            obs_noise.reshape(1, OD), perturbation,
        )
    ]
    system, prior_all = pl.pallas_call(
        predict_kernel,
        out_shape=(
            jax.ShapeDtypeStruct((2 * NE, NE), F32),
            jax.ShapeDtypeStruct((NY, MD, PD), BF16),
        ),
        in_specs=[hbm] * 7,
        out_specs=(vmem, anywhere),
        scratch_shapes=[
            pltpu.VMEM((NB, KB), jnp.int32),
            pltpu.VMEM((4, 128), jnp.int32),
            pltpu.VMEM((1, OD), F32),
            pltpu.VMEM((1, OD), F32),
            pltpu.VMEM((MD, OD), F32),
            pltpu.VMEM((NB, KB, OB, PB), BF16),
            pltpu.VMEM((MD, PD), F32),
            pltpu.VMEM((MD, PD), BF16),
            pltpu.VMEM((NB * KB // 2 * MD, 128), F32),
            pltpu.VMEM((NQ, 256, 256), BF16),
            pltpu.VMEM((2, 8, 128), F32),
            pltpu.VMEM((256, 128), F32),
            pltpu.VMEM((256, 256), BF16),
            pltpu.VMEM((NQ, NX, NZ, 16, 128), BF16),
            pltpu.VMEM((NQ, NX - 1, NZ, 16, 128), BF16),
            pltpu.VMEM((NQ, NX - 1, 16, 128), BF16),
            pltpu.VMEM((NQ, NZ - 1, 16, 128), BF16),
            pltpu.VMEM((NQ, NZ - 1, NX, 16, 128), BF16),
            pltpu.VMEM((NQ, NZ, 16, 128), BF16),
            pltpu.VMEM((NY * 128, 128), F32),
            pltpu.VMEM((NY, MD, OD), F32),
            pltpu.VMEM((NE, OD), F32),
            pltpu.VMEM((NE, OD), F32),
            pltpu.VMEM((NC * NX, 8, 128), F32),
            pltpu.VMEM((NC * NX, 8, 128), F32),
            pltpu.VMEM((NZ, 8, 128), F32),
            dma((NB // 2,)), dma, dma((5,)), dma,
            dma((2,)), dma((2,)),
            dma((NQ + 1,)), dma((NQ + 1,)),
            dma((NQ,)), dma((NQ,)),
            dma((NQ,)), dma((NQ,)),
            dma((NQ,)), dma((NQ,)),
            dma((3,)), dma((3,)),
        ],
        compiler_params=pltpu.CompilerParams(
            collective_id=0, has_side_effects=True, vmem_limit_bytes=40 * 2**20
        ),
        name="predict",
    )(*operands)
    return pl.pallas_call(
        solve_kernel,
        out_shape=(
            jax.ShapeDtypeStruct((MD, PD), F32),
            jax.ShapeDtypeStruct((NE, NE), F32),
        ),
        in_specs=[vmem, vmem],
        out_specs=(anywhere, anywhere),
        scratch_shapes=[
            pltpu.VMEM((NE, NE), F32),
            pltpu.VMEM((NE, NE), F32),
            pltpu.VMEM((NE, NE), F32),
            pltpu.VMEM((4, MD, 1024), F32),
            dma((5,)),
        ],
        compiler_params=pltpu.CompilerParams(vmem_limit_bytes=24 * 2**20),
        name="solve",
    )(system, prior_all)


def solution(mesh):
    return jax.shard_map(
        local,
        mesh=mesh,
        in_specs=(
            P("member", ("slab", "tile")),
            P(("slab", "tile"), None, None, None),
            P(("slab", "tile"), None),
            P(),
            P(("slab", "tile")),
            P(("slab", "tile")),
            P("member", ("slab", "tile")),
        ),
        out_specs=(P("member", ("slab", "tile")), P()),
        check_vma=False,
    )
```

```python
import functools
import math

import jax
import jax.numpy as jnp
from jax import lax
from jax.experimental import pallas as pl
from jax.experimental.pallas import tpu as pltpu
from jax.sharding import PartitionSpec as P

MESH = pl.DeviceIdType.MESH
F32, BF16 = jnp.float32, jnp.bfloat16
HIGHEST = lax.Precision.HIGHEST

NY, NC, NX, NZ = 4, 2, 4, 8
MD = 32
NB, KB, OB, PB = 8, 16, 64, 512
PD = NB * PB
OD = 8 * OB
NE = NY * MD
NT = NX * NZ
NQ = 8
X_FIRST, Z_FIRST = ((0, 1), (1, 2), (3, 2), (5, 1)), ((6, 2),)
PLACE = ((0, 1), (6, 2), (1, 2), (3, 2), (5, 1))
SUMS = (
    (0, (0, 1)), (0, (1, 2)), (0, (6, 2)), (0, (3, 2)), (1, (0, 1)), (0, (5, 1)),
    (1, (1, 2)), (1, (6, 2)), (1, (3, 2)), (1, (5, 1)),
)
NORM = 1.0 / math.sqrt(NE - 1)


def rows_contract(a, b, precision=None):
    return lax.dot_general(
        a, b, (((1,), (1,)), ((), ())), precision=precision, preferred_element_type=F32
    )


def predict_kernel(
    prior_hbm, sens_hbm, pattern_hbm, own_hbm, obs_hbm, noise_hbm, pert_hbm,
    sys_ref, prior_all,
    pattern_ref, own_ref, obs_ref, noise_ref, pert_ref,
    sens_v, prior_v, prior_bf, t_buf, u_buf, pat_buf, owner, onehot, placed, x_in, x_own, z_in, z_all, first_sum,
    pred, pert_all, s_buf, d_buf, part, ab_in, c_in,
    load_sem, prior_sem, small_sem, own_sem, g_send, g_recv, u_send, u_recv, x_send, x_recv, z_send, z_recv,
    y_send, y_recv, r_send, r_recv,
):
    y, c, t = lax.axis_index("member"), lax.axis_index("slab"), lax.axis_index("tile")
    x, z = lax.div(t, NZ), lax.rem(t, NZ)

    def wrap(v, n):
        return lax.rem(v, n)

    def device(dy, dc, dx, dz):
        return (wrap(y + dy, NY), wrap(c + dc, NC), wrap(x + dx, NX) * NZ + wrap(z + dz, NZ))

    def send(src, dst, send_sem, recv_sem, to):
        pltpu.make_async_remote_copy(
            src_ref=src, dst_ref=dst, send_sem=send_sem, recv_sem=recv_sem,
            device_id=to, device_id_type=MESH,
        ).start()

    def wait(ref, sem):
        pltpu.make_async_copy(ref, ref, sem).wait()

    started = set()
    arrivals, ends = {}, []

    def expect(name, ref, send_sem, recv_sem):
        arrivals[name] = (ref, recv_sem)
        started.add(name)
        ends.append((ref, send_sem))

    def arrive(name):
        wait(*arrivals.pop(name))

    def finish():
        for name in list(arrivals):
            arrive(name)
        while ends:
            wait(*ends.pop())
        if "prior" in started:
            keep_prior.wait()

    load_prior = pltpu.make_async_copy(prior_hbm, prior_v, prior_sem)
    load_prior.start()
    loads = [
        pltpu.make_async_copy(sens_hbm.at[pl.ds(2 * i, 2)], sens_v.at[pl.ds(2 * i, 2)], load_sem.at[i])
        for i in range(NB // 2)
    ]
    small = [
        pltpu.make_async_copy(src, dst, small_sem.at[i])
        for i, (src, dst) in enumerate((
            (pattern_hbm, pattern_ref), (pert_hbm, pert_ref), (own_hbm, own_ref), (obs_hbm, obs_ref),
            (noise_hbm, noise_ref),
        ))
    ]
    small[0].start()
    for load in loads:
        load.start()
    for load in small[1:]:
        load.start()

    column = [(dy, dc, dx) for dy in range(NY) for dc in range(NC) for dx in range(NX)][1:]
    barrier = pltpu.get_barrier_semaphore()
    for dy, dc, dx in column:
        pl.semaphore_signal(barrier, inc=1, device_id=device(dy, dc, dx, 0), device_id_type=MESH)
    for dz in range(1, NZ):
        pl.semaphore_signal(barrier, inc=1, device_id=device(0, 0, 0, dz), device_id_type=MESH)

    small[0].wait()
    j = lax.broadcasted_iota(jnp.int32, (KB, 128), 1)
    k = lax.broadcasted_iota(jnp.int32, (KB, 128), 0)
    pick = (k == 2 * (j & 7) + ((j >> 4) & 1)).astype(F32)
    spread_rows = jnp.dot(pattern_ref[...].astype(F32), pick, precision=HIGHEST, preferred_element_type=F32)
    j = lax.broadcasted_iota(jnp.int32, (NB, 128), 1)
    b = lax.broadcasted_iota(jnp.int32, (NB, 128), 0)
    row = jnp.sum(
        jnp.where(b == 2 * (j >> 5) + ((j >> 3) & 1), spread_rows, 0.0), axis=0, keepdims=True
    )
    pat_buf[0] = jnp.broadcast_to(row, (8, 128))

    load_prior.wait()
    prior_bf[...] = prior_v[...].astype(BF16)
    low = lax.broadcasted_iota(jnp.int32, (16, 128), 1) < OB

    def slots(i):
        for r in range(MD // 2):
            ta = t_buf[pl.ds(i * 16 * MD + r, 16, stride=MD), :]
            tb = t_buf[pl.ds(i * 16 * MD + r + 16, 16, stride=MD), :]
            lanes = pl.ds(r % 2 * 128, 128)
            u_buf[r // 2, pl.ds(i * 32, 16), lanes] = jnp.where(low, ta, pltpu.roll(tb, OB, 1)).astype(BF16)
            u_buf[r // 2, pl.ds(i * 32 + 16, 16), lanes] = jnp.where(low, pltpu.roll(ta, OB, 1), tb).astype(BF16)

    def product(b):
        return rows_contract(prior_bf[:, b * PB : (b + 1) * PB], sens_v[b].reshape(KB * OB, PB))

    def keep(b, out):
        for kp in range(KB // 2):
            t_buf[pl.ds((b * 8 + kp) * MD, MD), :] = out[:, kp * 128 : (kp + 1) * 128]

    for i in range(NB // 2):
        loads[i].wait()
        out = product(2 * i)
        if i:
            slots(i - 1)
        keep(2 * i, out)
        keep(2 * i + 1, product(2 * i + 1))
    slots(NB // 2 - 1)

    for load in small[1:]:
        load.wait()
    for i in range(2):
        owned = own_ref[pl.ds(2 * c + i, 1), :].astype(F32)
        owned = jnp.broadcast_to(owned, (128, 128)).T
        owner[pl.ds(i * 128, 128), :] = owned
        onehot[pl.ds(i * 128, 128), pl.ds(0, 128)] = (owned == row).astype(F32).astype(BF16)
    pert_all[y] = pert_ref[...]

    pl.semaphore_wait(barrier, len(column) + NZ - 1)
    sibling = device(0, 1, 0, 0)
    send(pat_buf.at[0], pat_buf.at[1], u_send.at[NQ], u_recv.at[NQ], sibling)
    expect("pattern", pat_buf.at[1], u_send.at[NQ], u_recv.at[NQ])
    for group in PLACE:
        qs, at = pl.ds(*group), group[0]
        there = u_buf.at[qs, pl.ds(128, 128)]
        send(u_buf.at[qs, pl.ds(0, 128)], there, u_send.at[at], u_recv.at[at], sibling)
        expect(("u", group), there, u_send.at[at], u_recv.at[at])
    for dy in range(1, NY):
        send(pert_ref, pert_all.at[y], g_send.at[0], g_recv.at[0], device(dy, 0, 0, 0))
    expect("pert", pert_all.at[pl.ds(0, NY - 1)], g_send.at[0], g_recv.at[0])
    for dy in range(1, NY):
        send(prior_bf, prior_all.at[y], g_send.at[1], g_recv.at[1], device(dy, 0, 0, 0))
    expect("prior", prior_all.at[pl.ds(0, NY - 1)], g_send.at[1], g_recv.at[1])
    keep_prior = pltpu.make_async_copy(prior_bf, prior_all.at[y], own_sem)
    keep_prior.start()
    arrive("pattern")
    onehot[:, pl.ds(128, 128)] = (owner[...] == pat_buf[1, 0:1, :]).astype(F32).astype(BF16)

    def place(group):
        arrive(("u", group))
        for q in range(group[0], sum(group)):
            out = jnp.dot(onehot[...], u_buf[q], preferred_element_type=F32)
            out = jnp.concatenate(
                [out[:, :128].reshape(NX, NZ, 8, 128), out[:, 128:].reshape(NX, NZ, 8, 128)], axis=2
            )
            placed[q] = out.astype(BF16)

    x_land = {g: (x_in if g in X_FIRST else x_own) for g in X_FIRST + Z_FIRST}
    z_land = {g: (z_all if g in Z_FIRST else z_in) for g in X_FIRST + Z_FIRST}

    def send_x(group):
        qs, land = pl.ds(*group), x_land[group]
        for dx in range(1, NX):
            to = wrap(x + dx, NX)
            src = placed.at[qs, to] if group in X_FIRST else first_sum.at[qs, to]
            send(src, land.at[qs, dx - 1], x_send.at[group[0]], x_recv.at[group[0]], device(0, 0, dx, 0))
        expect(("x", group), land.at[qs], x_send.at[group[0]], x_recv.at[group[0]])

    def send_z(group):
        qs, land = pl.ds(*group), z_land[group]
        for dz in range(1, NZ):
            to = wrap(z + dz, NZ)
            src = placed.at[qs, :, to] if group in Z_FIRST else first_sum.at[qs, to]
            send(src, land.at[qs, dz - 1], z_send.at[group[0]], z_recv.at[group[0]], device(0, 0, 0, dz))
        expect(("z", group), land.at[qs], z_send.at[group[0]], z_recv.at[group[0]])

    def sum_first(group):
        if group in X_FIRST:
            arrive(("x", group))
            for q in range(group[0], sum(group)):
                total = placed[q, x].astype(F32)
                for d in range(NX - 1):
                    total += x_in[q, d].astype(F32)
                first_sum[q] = total.astype(BF16)
            send_z(group)
        else:
            arrive(("z", group))
            for q in range(group[0], sum(group)):
                total = placed[q, :, z].astype(F32)
                for d in range(NZ - 1):
                    total += z_all[q, d].astype(F32)
                first_sum[q, pl.ds(0, NX)] = total.astype(BF16)
            send_x(group)

    def sum_second(group):
        if group in X_FIRST:
            arrive(("z", group))
            parts, own = [z_in.at[:, d] for d in range(NZ - 1)], z
        else:
            arrive(("x", group))
            parts, own = [x_own.at[:, d] for d in range(NX - 1)], x
        for q in range(group[0], sum(group)):
            total = first_sum[q, own].astype(F32)
            for p in parts:
                total += p[q].astype(F32)
            pred[pl.ds(pl.multiple_of(y * 128 + q * 16, 16), 16), :] = total
        rows = pl.ds(pl.multiple_of(y * 128 + group[0] * 16, 16), group[1] * 16)
        for dy in range(1, NY):
            send(pred.at[rows], pred.at[rows], y_send.at[group[0]], y_recv.at[group[0]], device(dy, 0, 0, 0))
        expect(("y", group), pred.at[pl.ds(0, 48 * group[1])], y_send.at[group[0]], y_recv.at[group[0]])

    for group in PLACE:
        place(group)
        (send_x if group in X_FIRST else send_z)(group)

    for stage, group in SUMS:
        (sum_second if stage else sum_first)(group)
    arrive("pert")
    for group in X_FIRST + Z_FIRST:
        arrive(("y", group))

    low = lax.broadcasted_iota(jnp.int32, (NE // 2, 128), 1) < OB
    misfit = jnp.zeros((1, 1), F32)
    for n in range(OD // 128):
        even = pred[pl.ds(2 * n, NE // 2, stride=8), :]
        odd = pred[pl.ds(2 * n + 1, NE // 2, stride=8), :]
        first = jnp.where(low, even, pltpu.roll(odd, OB, 1))
        second = jnp.where(low, pltpu.roll(even, OB, 1), odd)
        pieces = []
        for w in range(NY):
            pieces += [first[w * 16 : (w + 1) * 16], second[w * 16 : (w + 1) * 16]]
        predicted = jnp.concatenate(pieces, axis=0)
        cols = pl.ds(n * 128, 128)
        noise = noise_ref[:, cols]
        mean = jnp.sum(predicted, axis=0, keepdims=True) / NE
        s_buf[:, cols] = (predicted - mean) * NORM / noise
        innovation = (obs_ref[:, cols] - predicted) / noise + pert_all[:, :, cols].reshape(NE, 128)
        d_buf[:, cols] = innovation
        misfit += jnp.sum(innovation * innovation, axis=(0, 1), keepdims=True)

    half = wrap(y, 2) * 64
    left = s_buf[pl.ds(pl.multiple_of(half, 64), 64), :]
    right = jnp.where(y < 2, s_buf[...], d_buf[...])
    quarter = rows_contract(left, right, HIGHEST)
    r_id = lax.broadcasted_iota(jnp.int32, (64, 128), 0) + half
    c_id = lax.broadcasted_iota(jnp.int32, (64, 128), 1)
    diagonal = jnp.logical_and(r_id == c_id, y < 2)
    quarter = quarter + jnp.where(diagonal, misfit / (4.0 * NE * NE), 0.0)
    part[...] = quarter.reshape(NC * NX, 8, 128)

    me = c * NX + x
    ab_in[me] = part[me]
    for dy, dc, dx in column:
        if dy == 0:
            to = wrap(c + dc, NC) * NX + wrap(x + dx, NX)
            send(part.at[to], ab_in.at[me], r_send.at[0], r_recv.at[0], device(0, dc, dx, 0))
    expect("ab", ab_in.at[pl.ds(0, NC * NX - 1)], r_send.at[0], r_recv.at[0])
    arrive("ab")
    total = ab_in[0]
    for n in range(1, NC * NX):
        total += ab_in[n]
    c_in[z] = total
    for dz in range(1, NZ):
        send(c_in.at[z], c_in.at[z], r_send.at[1], r_recv.at[1], device(0, 0, 0, dz))
    expect("c", c_in.at[pl.ds(0, NZ - 1)], r_send.at[1], r_recv.at[1])
    arrive("c")
    total = c_in[0]
    for n in range(1, NZ):
        total += c_in[n]
    rows = pl.ds(pl.multiple_of(y * 64 + me * 8, 8), 8)
    sys_ref[rows, :] = total
    for dy, dc, dx in column:
        send(sys_ref.at[rows], sys_ref.at[rows], r_send.at[2], r_recv.at[2], device(dy, dc, dx, 0))
    finish()
    expect("rows", sys_ref.at[pl.ds(0, 8 * len(column))], r_send.at[2], r_recv.at[2])
    arrive("rows")
    wait(*ends.pop())


def solve_kernel(
    sys_ref, prior_all, inc_hbm, weights_hbm, x_buf, w_buf, cen_buf, inc_buf, out_sem
):
    def mul(a, b):
        return jnp.dot(a, b, precision=HIGHEST, preferred_element_type=F32)

    def rough(a, b):
        return jnp.dot(a.astype(BF16), b.astype(BF16), preferred_element_type=F32)

    system, cross = sys_ref[:NE, :], sys_ref[NE:, :]
    eye = (
        lax.broadcasted_iota(jnp.int32, (NE, NE), 0) == lax.broadcasted_iota(jnp.int32, (NE, NE), 1)
    ).astype(F32)
    size = jnp.sum(jnp.abs(system), axis=0, keepdims=True)
    inverse = eye * (2.0 / (size + jnp.maximum(jnp.sum(system, axis=0, keepdims=True), 0.0)))
    for _ in range(2):
        inverse = inverse + rough(inverse, eye - rough(system, inverse))
    weights = rough(inverse, cross)
    for _ in range(2):
        weights = weights + rough(inverse, cross - mul(system, weights))
    residual = cross - mul(system, weights)
    y = lax.axis_index("member")
    stores = [pltpu.make_async_copy(w_buf, weights_hbm, out_sem.at[4])]
    for n in range(4):
        stores.append(pltpu.make_async_copy(inc_buf.at[n], inc_hbm.at[:, pl.ds(n * 1024, 1024)], out_sem.at[n]))

    def update(weights):
        w_buf[...] = weights
        stores[0].start()
        centred = (weights - jnp.sum(weights, axis=0, keepdims=True) / NE) * NORM
        cen_buf[...] = centred.T
        own = cen_buf[pl.ds(pl.multiple_of(y * MD, MD), MD), :].astype(BF16)
        for n in range(4):
            cols = pl.ds(n * 1024, 1024)
            inc_buf[n] = jnp.dot(own, prior_all[:, :, cols].reshape(NE, 1024), preferred_element_type=F32)
            stores[n + 1].start()

    update(weights)

    @pl.when(jnp.logical_not(jnp.sum(residual * residual) <= 1e-10 * jnp.sum(cross * cross)))
    def _():
        for store in stores:
            store.wait()
        x_buf[...] = eye / jnp.max(size, axis=1, keepdims=True)

        def step(carry):
            count, _ = carry
            inverse = x_buf[...]
            residual = eye - mul(sys_ref[:NE, :], inverse)
            x_buf[...] = inverse + mul(inverse, residual)
            return count + 1, jnp.sum(residual * residual)

        lax.while_loop(
            lambda carry: jnp.logical_and(carry[0] < 64, carry[1] > 1e-7), step, (0, jnp.float32(1.0))
        )
        weights = mul(x_buf[...], sys_ref[NE:, :])
        for _ in range(2):
            weights = weights + mul(x_buf[...], sys_ref[NE:, :] - mul(sys_ref[:NE, :], weights))
        update(weights)

    for store in stores:
        store.wait()


def local(prior, sensitivity, pattern, ownership, observed, obs_noise, perturbation):
    vmem, anywhere = pl.BlockSpec(memory_space=pltpu.VMEM), pl.BlockSpec(memory_space=pl.ANY)
    hbm = pl.BlockSpec(memory_space=pltpu.HBM)
    dma = pltpu.SemaphoreType.DMA
    operands = [
        pltpu.with_memory_space_constraint(a, pltpu.HBM)
        for a in (
            prior, sensitivity, pattern, ownership.reshape(4, 128), observed.reshape(1, OD),
            obs_noise.reshape(1, OD), perturbation,
        )
    ]
    system, prior_all = pl.pallas_call(
        predict_kernel,
        out_shape=(
            jax.ShapeDtypeStruct((2 * NE, NE), F32),
            jax.ShapeDtypeStruct((NY, MD, PD), BF16),
        ),
        in_specs=[hbm] * 7,
        out_specs=(vmem, anywhere),
        scratch_shapes=[
            pltpu.VMEM((NB, KB), jnp.int32),
            pltpu.VMEM((4, 128), jnp.int32),
            pltpu.VMEM((1, OD), F32),
            pltpu.VMEM((1, OD), F32),
            pltpu.VMEM((MD, OD), F32),
            pltpu.VMEM((NB, KB, OB, PB), BF16),
            pltpu.VMEM((MD, PD), F32),
            pltpu.VMEM((MD, PD), BF16),
            pltpu.VMEM((NB * KB // 2 * MD, 128), F32),
            pltpu.VMEM((NQ, 256, 256), BF16),
            pltpu.VMEM((2, 8, 128), F32),
            pltpu.VMEM((256, 128), F32),
            pltpu.VMEM((256, 256), BF16),
            pltpu.VMEM((NQ, NX, NZ, 16, 128), BF16),
            pltpu.VMEM((NQ, NX - 1, NZ, 16, 128), BF16),
            pltpu.VMEM((NQ, NX - 1, 16, 128), BF16),
            pltpu.VMEM((NQ, NZ - 1, 16, 128), BF16),
            pltpu.VMEM((NQ, NZ - 1, NX, 16, 128), BF16),
            pltpu.VMEM((NQ, NZ, 16, 128), BF16),
            pltpu.VMEM((NY * 128, 128), F32),
            pltpu.VMEM((NY, MD, OD), F32),
            pltpu.VMEM((NE, OD), F32),
            pltpu.VMEM((NE, OD), F32),
            pltpu.VMEM((NC * NX, 8, 128), F32),
            pltpu.VMEM((NC * NX, 8, 128), F32),
            pltpu.VMEM((NZ, 8, 128), F32),
            dma((NB // 2,)), dma, dma((5,)), dma,
            dma((2,)), dma((2,)),
            dma((NQ + 1,)), dma((NQ + 1,)),
            dma((NQ,)), dma((NQ,)),
            dma((NQ,)), dma((NQ,)),
            dma((NQ,)), dma((NQ,)),
            dma((3,)), dma((3,)),
        ],
        compiler_params=pltpu.CompilerParams(
            collective_id=0, has_side_effects=True, vmem_limit_bytes=40 * 2**20
        ),
        name="predict",
    )(*operands)
    return pl.pallas_call(
        solve_kernel,
        out_shape=(
            jax.ShapeDtypeStruct((MD, PD), F32),
            jax.ShapeDtypeStruct((NE, NE), F32),
        ),
        in_specs=[vmem, vmem],
        out_specs=(anywhere, anywhere),
        scratch_shapes=[
            pltpu.VMEM((NE, NE), F32),
            pltpu.VMEM((NE, NE), F32),
            pltpu.VMEM((NE, NE), F32),
            pltpu.VMEM((4, MD, 1024), F32),
            dma((5,)),
        ],
        compiler_params=pltpu.CompilerParams(vmem_limit_bytes=24 * 2**20),
        name="solve",
    )(system, prior_all)


def solution(mesh):
    return jax.shard_map(
        local,
        mesh=mesh,
        in_specs=(
            P("member", ("slab", "tile")),
            P(("slab", "tile"), None, None, None),
            P(("slab", "tile"), None),
            P(),
            P(("slab", "tile")),
            P(("slab", "tile")),
            P("member", ("slab", "tile")),
        ),
        out_specs=(P("member", ("slab", "tile")), P()),
        check_vma=False,
    )
```
